256 devices in a mesh: fibre: 16 (over z_lo, y, core), band: 16 (over x, z_hi).
Axes of the slice: x: 4, y: 4, z: 8 (z_hi: 4, z_lo: 2; z = z_hi * 2 + z_lo), core: 2. Of those that a mesh axis runs over, the one named last changes fastest.
Arguments:
- spectra: bfloat16 [2, 32, 512, 2048], P(None, None, 'band', 'fibre'), may hold values from -6 to 6
- dead_mask: int32 [2048], P('fibre'), may hold values 0 or 1
- partner_offset: int32 [16, 4], P('fibre'), may hold values from 0 to 8, as said below
Outputs:
- correlations: bfloat16 [32, 16, 4, 128, 128], P('band', 'fibre')
The draws below stay inside these ranges and needn't reach their ends.
Inputs may be any that keep to these rules, and one draw needn't show every extreme that they name: `partner_offset`: A block's partner is itself or a later block, never past the last block; slot 0 holds the farthest partner allowed, min(8, 15 - b).
All inputs are finite; a program needn't handle non-finite values. No bound on the sum of `dead_mask` on one device may be relied on, other than what follows from the above.
Results may differ from the reference program's by a relative error of at most 0.0045.
Values may be sent and summed in bfloat16 or wider, within the bound.
A program may use at most 128 MiB of HBM per device.

```python
import math
import jax
import jax.numpy as jnp
from jax import lax

BS = 128
NF = 512
REACH = 8
K = 4
W = 32
LAGS = 32
BLOCKS = 16
CHANNELS = 2048


def draw_partner_offset(key, part):
    key = jax.random.fold_in(key, 7)
    block_index = jnp.arange(BLOCKS, dtype=jnp.int32)
    limits = jnp.minimum(REACH, BLOCKS - 1 - block_index)
    random_words = jax.random.randint(key, (BLOCKS, K), 0, 1 << 20, dtype=jnp.int32)
    offsets = random_words % (limits[:, None] + 1)
    slot_index = jnp.arange(K, dtype=jnp.int32)[None, :]
    offsets = jnp.where(slot_index == 0, limits[:, None], offsets)
    return offsets.astype(jnp.int32)


def touch_ends(drawn, stream_key, smallest, top_value):
    shape = drawn.shape
    place = [jax.random.randint(jax.random.fold_in(stream_key, axis), (), 0, shape[axis]) for axis in range(len(shape))]
    drawn = drawn.at[tuple(place)].set(smallest)
    longest = shape.index(max(shape))
    place[longest] = (place[longest] + 1) % shape[longest]
    return drawn.at[tuple(place)].set(top_value)


def steps_of(stream_key, extent, cuts, smallest, largest):
    factor_of, own = 1.0, jax.random.fold_in(stream_key, 6)
    for position, parts in cuts:
        steps = jnp.exp(jax.random.uniform(jax.random.fold_in(own, position), (parts,), jnp.float32, smallest / len(cuts), largest / len(cuts)))
        factor_of = factor_of * jnp.repeat(steps, extent[position] // parts).reshape([-1 if axis == position else 1 for axis in range(len(extent))])
    return factor_of


def normal_values(key, shape, scale, bound, shards=(), kind=jnp.bfloat16):
    entries = jax.random.normal(key, shape, jnp.float32) * scale
    if len(shards) > 0:
        entries = steps_of(key, shape, shards, -0.22, 0.18) * entries
    return jnp.clip(entries, min=-bound, max=bound).astype(kind)


def setup_inputs(seed: int = 0) -> dict:
    keys = jax.random.split(jax.random.key(seed), 4)
    spectra = normal_values(keys[0], (2, W, NF, CHANNELS), 1.0, 6.0, ((2, 16), (3, 16)))
    dead_mask = touch_ends((jax.random.randint(keys[1], (CHANNELS,), 0, 8) < 7).astype(jnp.int32), jax.random.fold_in(keys[1], 1), 0, 1)
    partner_offset = draw_partner_offset(jax.random.fold_in(keys[3], 71), 0)
    return dict(spectra=spectra, dead_mask=dead_mask, partner_offset=partner_offset)


def make_table(freq_index):
    lag_index = jnp.arange(LAGS, dtype=jnp.int32) - LAGS // 2
    phases = freq_index[:, None] * lag_index[None, :] % (2 * NF)
    angles = phases.astype(jnp.float32) * (math.pi / NF)
    return jnp.stack([jnp.cos(angles), -jnp.sin(angles)], axis=1).astype(jnp.bfloat16)

def pair_correlation(masked, table, first_block, second_block):
    own_block = lax.dynamic_slice_in_dim(masked, (first_block * BS).astype(jnp.int32), BS, 3)
    other_block = lax.dynamic_slice_in_dim(masked, (second_block * BS).astype(jnp.int32), BS, 3)
    left_side = jnp.concatenate([jnp.concatenate([own_block[0], own_block[1]], axis=0), jnp.concatenate([own_block[1], -own_block[0]], axis=0)], axis=2)
    right_side = jnp.concatenate([other_block[0], other_block[1]], axis=0)
    products = jnp.einsum('wfi,wfj->fij', left_side.astype(jnp.float32), right_side.astype(jnp.float32), precision=lax.Precision.HIGHEST)
    cross = (products * (1.0 / math.sqrt(W))).astype(jnp.bfloat16).reshape(NF, 2, BS, BS)
    lagged = jnp.einsum('frl,frij->lij', table.astype(jnp.float32), cross.astype(jnp.float32), precision=lax.Precision.HIGHEST)
    return (lagged * (1.0 / math.sqrt(NF))).astype(jnp.bfloat16)

def reference(spectra, dead_mask, partner_offset):
    masked = spectra * dead_mask.astype(jnp.bfloat16)[None, None, None, :]
    table = make_table(jnp.arange(NF, dtype=jnp.int32))
    first_blocks = jnp.repeat(jnp.arange(BLOCKS, dtype=jnp.int32), K)
    second_blocks = first_blocks + partner_offset.reshape(-1).astype(jnp.int32)

    def one_pair(pair_ids):
        return pair_correlation(masked, table, pair_ids[0], pair_ids[1])
    stacked = lax.map(one_pair, (first_blocks, second_blocks))
    return stacked.reshape(BLOCKS, K, LAGS, BS, BS).transpose(2, 0, 1, 3, 4)
```

```python
import math

import jax
import jax.numpy as jnp
import ml_dtypes
import numpy as np
from jax import lax
from jax.experimental import pallas as pl
from jax.experimental.pallas import tpu as pltpu
from jax.sharding import PartitionSpec as P

BS = 128
NF = 512
REACH = 8
K = 4
W = 32
LAGS = 32
BANDS = 16
BINS = NF // BANDS
DEPTH = 2 * W * BINS
HALF = W * BINS
CHUNKS = 4
CROWS = DEPTH // CHUNKS
TILE = 256
XROWS = LAGS // 4 * BS
ZROWS = LAGS // 16 * BS
SCALE = 1.0 / math.sqrt(W) / math.sqrt(NF)


def lag_table():
    bins = np.arange(NF)[:, None]
    lags = np.arange(LAGS)[None, :] - LAGS // 2
    angles = (bins * lags % (2 * NF)) * (math.pi / NF)
    table = np.stack([np.cos(angles), -np.sin(angles)], axis=2)
    table = table.astype(np.float32).astype(ml_dtypes.bfloat16).astype(np.float32)
    table = table.reshape(BANDS, BINS, 2 * LAGS).transpose(0, 2, 1)
    return np.tile(table, (1, 1, BS // BINS))


def kernel(
    spectra, mask, offsets, table, out,
    blocks, turned, left, right, sums, own, got, zsums, zown, zgot,
    gather_send, gather_recv, sib_send, x_send, x_recv, z_send, z_recv,
):
    fibre, band = lax.axis_index("fibre"), lax.axis_index("band")
    z_lo, y, core = fibre // 8, fibre // 2 % 4, fibre % 2
    chip = fibre // 2
    x, z_hi = band // 4, band % 4

    def at_fibre(zz, yy, cc):
        return {"fibre": (zz * 4 + yy) * 2 + cc, "band": band}

    def at_band(xx, zz):
        return {"fibre": fibre, "band": xx * 4 + zz}

    sibling = at_fibre(z_lo, y, 1 - core)
    barrier = pltpu.get_barrier_semaphore()
    peers = [sibling, at_fibre(1 - z_lo, y, core)]
    peers += [at_fibre(z_lo, (y + j) % 4, core) for j in (1, 2, 3)]
    peers += [at_band((x + j) % 4, z_hi) for j in (1, 2, 3)]
    peers += [at_band(x, (z_hi + j) % 4) for j in (1, 2, 3)]
    for peer in peers:
        pl.semaphore_signal(barrier, inc=1, device_id=peer, device_id_type=pl.DeviceIdType.MESH)

    alive = mask[...].astype(jnp.bfloat16)
    blocks[0] = spectra[...] * alive
    pl.semaphore_wait(barrier, len(peers))

    def remote(src, dst, send, recv, device):
        return pltpu.make_async_remote_copy(
            src_ref=src, dst_ref=dst, send_sem=send, recv_sem=recv,
            device_id=device, device_id_type=pl.DeviceIdType.MESH,
        )

    def rows_of(ch):
        return pl.ds(ch * CROWS, CROWS)

    def far(ch):
        return remote(
            blocks.at[0, rows_of(ch)], blocks.at[8, rows_of(ch)],
            gather_send.at[3, ch], gather_recv.at[8, ch], at_fibre(1 - z_lo, y, core),
        )

    def near(j, ch):
        src = jnp.where(y >= j, 0, 8)
        return remote(
            blocks.at[src, rows_of(ch)], blocks.at[2 * j, rows_of(ch)],
            gather_send.at[j - 1, ch], gather_recv.at[2 * j, ch], at_fibre(z_lo, (y - j + 4) % 4, core),
        )

    def across(j, ch):
        return remote(
            blocks.at[2 * j + 2 * (1 - core), rows_of(ch)], blocks.at[2 * j + 1, rows_of(ch)],
            sib_send.at[j, ch], gather_recv.at[2 * j + 1, ch], sibling,
        )

    across_here = [chip + j + (1 - core) <= 7 for j in range(4)]
    across_there = [chip + j + core <= 7 for j in range(4)]
    even_here = [chip + j <= 7 for j in range(5)]

    @pl.when(z_lo == 1)
    def _():
        for ch in range(CHUNKS):
            far(ch).start()

    for j in (1, 2, 3):
        @pl.when(y >= j)
        def _(j=j):
            for ch in range(CHUNKS):
                near(j, ch).start()

    @pl.when(core == 1)
    def _():
        for ch in range(CHUNKS):
            across(0, ch).start()

    for r in range(2):
        for g in range(HALF // BS):
            piece = blocks[0, pl.ds(r * HALF + g * BS, BS), :].astype(jnp.float32)
            turned[r, :, pl.ds(g * BS, BS)] = piece.T

    def build(lag, carry):
        t0 = table[pl.ds(2 * lag, 1), :]
        t1 = table[pl.ds(2 * lag + 1, 1), :]
        rows = pl.ds(pl.multiple_of(lag * BS, BS), BS)
        for g in range(HALF // BS):
            re = turned[0, :, pl.ds(g * BS, BS)]
            im = turned[1, :, pl.ds(g * BS, BS)]
            left[rows, pl.ds(g * BS, BS)] = (t0 * re + t1 * im).astype(jnp.bfloat16)
            left[rows, pl.ds(HALF + g * BS, BS)] = (t0 * im - t1 * re).astype(jnp.bfloat16)
        return carry

    for ch in range(CHUNKS):
        lax.fori_loop(ch * LAGS // CHUNKS, (ch + 1) * LAGS // CHUNKS, build, 0)

        @pl.when(z_lo == 0)
        def _(ch=ch):
            far(ch).wait_recv()
            for j in (1, 2, 3):
                @pl.when(y < j)
                def _(j=j):
                    near(j, ch).start()

            @pl.when(core == 0)
            def _():
                across(3, ch).start()

    def pass_on(j):
        @pl.when(even_here[j])
        def _():
            for ch in range(CHUNKS):
                near(j, ch).wait_recv()

        send_j = j - 1 + core

        @pl.when(jnp.logical_and(chip + j <= 7, send_j <= 3))
        def _():
            for ch in range(CHUNKS):
                across(send_j, ch).start()

    def gather_rest():
        for j in (1, 2, 3):
            pass_on(j)
        for j in range(4):
            @pl.when(across_there[j])
            def _(j=j):
                for ch in range(CHUNKS):
                    across(j, ch).wait_recv()

    def x_copy(k, dd):
        return remote(
            sums.at[k, dd - 1], got.at[k, dd - 1], x_send.at[k, dd - 1], x_recv.at[k, dd - 1],
            at_band((x + dd) % 4, z_hi),
        )

    def z_copy(k, ee):
        return remote(
            zsums.at[k, ee - 1], zgot.at[k, ee - 1], z_send.at[k, ee - 1], z_recv.at[k, ee - 1],
            at_band(x, (z_hi + ee) % 4),
        )

    def multiply(k):
        for dd in (2, 1, 3, 0):
            base = (x + dd) % 4 * XROWS

            def tile(t, carry, dd=dd, base=base):
                here = pl.ds(pl.multiple_of(t * TILE, TILE), TILE)
                rows = pl.ds(pl.multiple_of(base + t * TILE, TILE), TILE)
                total = jnp.dot(left[rows, :], right[...], preferred_element_type=jnp.float32)
                if dd == 0:
                    own[k, here, :] = total
                else:
                    sums[k, dd - 1, here, :] = total.astype(jnp.bfloat16)
                return carry

            lax.fori_loop(0, XROWS // TILE, tile, 0)
            if dd != 0:
                x_copy(k, dd).start()

    def reduce_x(k):
        for dd in (1, 3, 2):
            x_copy(k, dd).wait_recv()
        for ee in (2, 1, 3, 0):
            rows = pl.ds(pl.multiple_of((z_hi + ee) % 4 * ZROWS, ZROWS), ZROWS)
            total = own[k, rows, :]
            for s in range(3):
                total += got[k, s, rows, :].astype(jnp.float32)
            if ee == 0:
                zown[k] = total
            else:
                zsums[k, ee - 1] = total.astype(jnp.bfloat16)
                z_copy(k, ee).start()

    def finish(k):
        for ee in (1, 3, 2):
            z_copy(k, ee).wait_recv()
        total = zown[k]
        for s in range(3):
            total += zgot[k, s].astype(jnp.float32)
        done = (total * SCALE).astype(jnp.bfloat16)
        for lag in range(2):
            out[lag, 0, k] = done[lag * BS:(lag + 1) * BS]

    @pl.when(z_lo == 1)
    def _():
        gather_rest()

    right[...] = blocks[jnp.minimum(REACH, 15 - fibre)]
    multiply(0)

    @pl.when(z_lo == 0)
    def _():
        gather_rest()

    right[...] = blocks[offsets[0, 1]]
    multiply(1)
    reduce_x(0)
    right[...] = blocks[offsets[0, 2]]
    multiply(2)
    reduce_x(1)
    finish(0)
    right[...] = blocks[offsets[0, 3]]
    multiply(3)
    reduce_x(2)
    finish(1)
    reduce_x(3)
    finish(2)
    finish(3)

    @pl.when(z_lo == 1)
    def _():
        for ch in range(CHUNKS):
            far(ch).wait_send()

    for j in (1, 2, 3):
        @pl.when(jnp.logical_or(y >= j, z_lo == 0))
        def _(j=j):
            for ch in range(CHUNKS):
                near(j, ch).wait_send()

    for j in range(4):
        @pl.when(across_here[j])
        def _(j=j):
            for ch in range(CHUNKS):
                across(j, ch).wait_send()

    for k in range(K):
        for dd in (1, 2, 3):
            x_copy(k, dd).wait_send()
            z_copy(k, dd).wait_send()


def on_device(spectra, dead_mask, partner_offset):
    table = lax.dynamic_index_in_dim(jnp.asarray(lag_table()), lax.axis_index("band"), 0, False)
    vmem = pl.BlockSpec(memory_space=pltpu.VMEM)
    bf16, f32 = jnp.bfloat16, jnp.float32
    return pl.pallas_call(
        kernel,
        out_shape=jax.ShapeDtypeStruct((LAGS // BANDS, 1, K, BS, BS), bf16),
        in_specs=[vmem, vmem, pl.BlockSpec(memory_space=pltpu.SMEM), vmem],
        out_specs=vmem,
        scratch_shapes=[
            pltpu.VMEM((REACH + 1, DEPTH, BS), bf16),
            pltpu.VMEM((2, BS, HALF), f32),
            pltpu.VMEM((LAGS * BS, DEPTH), bf16),
            pltpu.VMEM((DEPTH, BS), bf16),
            pltpu.VMEM((K, 3, XROWS, BS), bf16),
            pltpu.VMEM((K, XROWS, BS), f32),
            pltpu.VMEM((K, 3, XROWS, BS), bf16),
            pltpu.VMEM((K, 3, ZROWS, BS), bf16),
            pltpu.VMEM((K, ZROWS, BS), f32),
            pltpu.VMEM((K, 3, ZROWS, BS), bf16),
            pltpu.SemaphoreType.DMA((4, CHUNKS)),
            pltpu.SemaphoreType.DMA((REACH + 1, CHUNKS)),
            pltpu.SemaphoreType.DMA((4, CHUNKS)),
            pltpu.SemaphoreType.DMA((K, 3)),
            pltpu.SemaphoreType.DMA((K, 3)),
            pltpu.SemaphoreType.DMA((K, 3)),
            pltpu.SemaphoreType.DMA((K, 3)),
        ],
        compiler_params=pltpu.CompilerParams(
            collective_id=0, has_side_effects=True, vmem_limit_bytes=56 * 1024 * 1024
        ),
        cost_estimate=pl.CostEstimate(
            flops=2 * LAGS * BS * DEPTH * K * BS, bytes_accessed=1 << 20, transcendentals=0
        ),
    )(spectra.reshape(DEPTH, BS), dead_mask.reshape(1, BS), partner_offset, table)


def solution(mesh):
    in_specs = (P(None, None, "band", "fibre"), P("fibre"), P("fibre", None))
    out_specs = P("band", "fibre", None, None, None)
    return jax.shard_map(
        on_device, mesh=mesh, in_specs=in_specs, out_specs=out_specs, check_vma=False
    )
```

```python
import math

import jax
import jax.numpy as jnp
import ml_dtypes
import numpy as np
from jax import lax
from jax.experimental import pallas as pl
from jax.experimental.pallas import tpu as pltpu
from jax.sharding import PartitionSpec as P

BS = 128
NF = 512
REACH = 8
K = 4
W = 32
LAGS = 32
BANDS = 16
BINS = NF // BANDS
DEPTH = 2 * W * BINS
HALF = W * BINS
CHUNKS = 4
CROWS = DEPTH // CHUNKS
XROWS = LAGS // 4 * BS
HX = XROWS // 2
ZROWS = LAGS // 16 * BS
TAIL = 16
SCALE = 1.0 / math.sqrt(W) / math.sqrt(NF)


def lag_table():
    bins = np.arange(NF)[:, None]
    lags = np.arange(LAGS)[None, :] - LAGS // 2
    angles = (bins * lags % (2 * NF)) * (math.pi / NF)
    table = np.stack([np.cos(angles), -np.sin(angles)], axis=2)
    table = table.astype(np.float32).astype(ml_dtypes.bfloat16).astype(np.float32)
    table = table.reshape(BANDS, BINS, 2 * LAGS).transpose(0, 2, 1)
    return np.tile(table, (1, 1, BS // BINS))


def kernel(
    spectra, mask, offsets, tables, out,
    blocks, turned, left, right, table, part, go, come, zsums, zgot,
    table_sem, gather_send, relay_send, gather_recv, sib_send, x_send, x_recv, z_send, z_recv,
):
    fibre, band = lax.axis_index("fibre"), lax.axis_index("band")
    z_lo, y, core = fibre // 8, fibre // 2 % 4, fibre % 2
    chip = fibre // 2
    x, z_hi = band // 4, band % 4

    def at_fibre(zz, yy, cc):
        return {"fibre": (zz * 4 + yy) * 2 + cc, "band": band}

    def at_band(xx, zz):
        return {"fibre": fibre, "band": xx * 4 + zz}

    sibling = at_fibre(z_lo, y, 1 - core)
    other_z = at_fibre(1 - z_lo, y, core)
    y_down, y_up = at_fibre(z_lo, (y + 3) % 4, core), at_fibre(z_lo, (y + 1) % 4, core)
    x_down, x_up = at_band((x + 3) % 4, z_hi), at_band((x + 1) % 4, z_hi)
    barrier = pltpu.get_barrier_semaphore()
    peers = [sibling, other_z, y_down, y_up, x_down, x_up]
    peers += [at_band(x, (z_hi + j) % 4) for j in (1, 2, 3)]
    for peer in peers:
        pl.semaphore_signal(barrier, inc=1, device_id=peer, device_id_type=pl.DeviceIdType.MESH)

    table_copy = pltpu.make_async_copy(tables.at[band], table, table_sem)
    table_copy.start()
    alive = mask[...].astype(jnp.bfloat16)
    blocks[0] = spectra[...] * alive
    pl.semaphore_wait(barrier, len(peers))

    def remote(src, dst, send, recv, device):
        return pltpu.make_async_remote_copy(
            src_ref=src, dst_ref=dst, send_sem=send, recv_sem=recv,
            device_id=device, device_id_type=pl.DeviceIdType.MESH,
        )

    def rows_of(ch):
        return pl.ds(ch * CROWS, CROWS)

    def far(ch):
        return remote(
            blocks.at[0, rows_of(ch)], blocks.at[8, rows_of(ch)],
            gather_send.at[0, ch], gather_recv.at[8, ch], other_z,
        )

    def near(j, ch):
        src = jnp.where(y >= j, 0, 8)
        return remote(
            blocks.at[src, rows_of(ch)], blocks.at[2 * j, rows_of(ch)],
            gather_send.at[j, ch], gather_recv.at[2 * j, ch], y_down if j == 1 else y_up,
        )

    def relay(j, ch):
        return remote(
            blocks.at[2 * j, rows_of(ch)], blocks.at[4, rows_of(ch)],
            relay_send.at[j // 2, ch], gather_recv.at[4, ch], y_down if j == 1 else y_up,
        )

    def across(j, ch):
        return remote(
            blocks.at[2 * j + 2 * (1 - core), rows_of(ch)], blocks.at[2 * j + 1, rows_of(ch)],
            sib_send.at[j, ch], gather_recv.at[2 * j + 1, ch], sibling,
        )

    def relays(j, ch):
        first = ch < CHUNKS // 2
        if j == 1:
            goes = jnp.logical_or(y == 1, y >= 2) if first else y == 1
        else:
            goes = y == 2 if first else y <= 2
        return jnp.logical_and(chip + j <= 7, goes)

    def near_goes(j):
        return jnp.logical_or(y >= j, jnp.logical_and(z_lo == 0, y != 3))

    @pl.when(z_lo == 1)
    def _():
        for ch in range(CHUNKS):
            far(ch).start()

    for j in (1, 3):
        @pl.when(y >= j)
        def _(j=j):
            for ch in range(CHUNKS):
                near(j, ch).start()

    @pl.when(core == 1)
    def _():
        for ch in range(CHUNKS):
            across(0, ch).start()

    def take_far(ch):
        far(ch).wait_recv()
        for j in (1, 3):
            @pl.when(y < j if j == 1 else y < 3)
            def _(j=j):
                near(j, ch).start()

        @pl.when(core == 0)
        def _():
            across(3, ch).start()

    def take(j, ch):
        @pl.when(chip + j <= 7)
        def _():
            remote(
                blocks.at[0, rows_of(ch)], blocks.at[2 * j, rows_of(ch)],
                gather_send.at[0, ch], gather_recv.at[2 * j, ch], y_up,
            ).wait_recv()
            if j != 2:
                @pl.when(relays(j, ch))
                def _():
                    relay(j, ch).start()
            across(j - 1 + core, ch).start()

    def build(lag, carry):
        t0 = table[pl.ds(2 * lag, 1), :]
        t1 = table[pl.ds(2 * lag + 1, 1), :]
        rows = pl.ds(pl.multiple_of(lag * BS, BS), BS)
        for g in range(HALF // BS):
            re = turned[0, :, pl.ds(g * BS, BS)]
            im = turned[1, :, pl.ds(g * BS, BS)]
            left[rows, pl.ds(g * BS, BS)] = (t0 * re + t1 * im).astype(jnp.bfloat16)
            left[rows, pl.ds(HALF + g * BS, BS)] = (t0 * im - t1 * re).astype(jnp.bfloat16)
        return carry

    def turn(g, carry):
        rows = pl.ds(pl.multiple_of(g * BS, BS), BS)
        for r in range(2):
            turned[r, :, rows] = blocks[0, pl.ds(pl.multiple_of(r * HALF + g * BS, BS), BS), :].astype(jnp.float32).T
        return carry

    lax.fori_loop(0, HALF // BS, turn, 0)
    table_copy.wait()
    lax.fori_loop(0, LAGS // 2, build, 0)

    def step(s):
        if s < CHUNKS:
            @pl.when(z_lo == 0)
            def _():
                take_far(s)
            take(1, s)
        if 1 <= s <= CHUNKS:
            take(3, s - 1)
        if 2 <= s:
            take(2, s - 2)

    for s in range(CHUNKS):
        step(s)
        lax.fori_loop(LAGS // 2 + s * LAGS // 8, LAGS // 2 + (s + 1) * LAGS // 8, build, 0)

    def siblings_done():
        for j in range(4):
            @pl.when(chip + j + core <= 7)
            def _(j=j):
                for ch in range(CHUNKS):
                    across(j, ch).wait_recv()

    def middle(k, way):
        return remote(
            go.at[k, way, 0], come.at[k, way, 0], x_send.at[k, way, 0], x_recv.at[k, way, 0],
            x_down if way else x_up,
        )

    def straight(k, way):
        return remote(
            go.at[k, way, 1], come.at[k, way, 1], x_send.at[k, way, 1], x_recv.at[k, way, 1],
            x_down if way else x_up,
        )

    def summed(k, way):
        return remote(
            go.at[k, way, 2], come.at[k, way, 2], x_send.at[k, way, 2], x_recv.at[k, way, 2],
            x_down if way else x_up,
        )

    def z_copy(k, ee):
        return remote(
            zsums.at[k, ee - 1], zgot.at[k, ee - 1], z_send.at[k, ee - 1], z_recv.at[k, ee - 1],
            at_band(x, (z_hi + ee) % 4),
        )

    square = (BS, BS)
    diagonal = lax.broadcasted_iota(jnp.int32, square, 0) == lax.broadcasted_iota(jnp.int32, square, 1)
    tail_row = lax.broadcasted_iota(jnp.int32, (TAIL, BS), 0)

    def pack(message, lags, value_of):
        tail = jnp.zeros((TAIL, BS), jnp.float32)
        for lag in range(lags):
            value = value_of(lag)
            rounded = value.astype(jnp.bfloat16)
            message[pl.ds(lag * BS, BS), :] = rounded
            rest = jnp.where(diagonal, value - rounded.astype(jnp.float32), 0.0)
            tail = jnp.where(tail_row == lag, jnp.sum(rest, axis=0, keepdims=True), tail)
        message[pl.ds(lags * BS, TAIL), :] = tail.astype(jnp.bfloat16)

    def unpack(message, lags, lag):
        tail = message[pl.ds(lags * BS, TAIL), :].astype(jnp.float32)[lag:lag + 1]
        return message[pl.ds(lag * BS, BS), :].astype(jnp.float32) + jnp.where(diagonal, tail, 0.0)

    def part_of(k, q, lag):
        return part[k, q, pl.ds(lag * BS, BS), :]

    def multiply(k, between=None):
        def quarter(q, carry):
            @pl.when(q == 3)
            def _():
                for way in (0, 1):
                    middle(k, way).wait_recv()
                    def both(lag, way=way):
                        return part_of(k, 1 + way, way * 4 + lag) + unpack(come.at[k, way, 0], 4, lag)

                    pack(go.at[k, way, 2], 4, both)
                    summed(k, way).start()

            ahead = jnp.where(q == 0, 2, jnp.where(q == 1, 1, jnp.where(q == 2, 3, 0)))
            rows = pl.ds(pl.multiple_of((x + ahead) % 4 * XROWS, XROWS), XROWS)
            part[k, q] = jnp.dot(left[rows, :], right[...], preferred_element_type=jnp.float32)

            @pl.when(q == 0)
            def _():
                for way in (0, 1):
                    pack(go.at[k, way, 0], 4, lambda lag, way=way: part_of(k, 0, way * 4 + lag))
                    middle(k, way).start()

            for way in (0, 1):
                @pl.when(q == 1 + way)
                def _(way=way):
                    pack(go.at[k, way, 1], 4, lambda lag: part_of(k, 1 + way, (1 - way) * 4 + lag))
                    straight(k, way).start()

            if between is not None:
                between(q)
            return carry

        lax.fori_loop(0, 4, quarter, 0)

    def reduce_x(k):
        for way in (0, 1):
            straight(k, way).wait_recv()
            summed(k, way).wait_recv()
        for lag in range(8):
            up = 2 if lag < 4 else 1
            total = part_of(k, 3, lag) + unpack(come.at[k, 0, up], 4, lag % 4)
            part[k, 3, pl.ds(lag * BS, BS), :] = total + unpack(come.at[k, 1, 3 - up], 4, lag % 4)
        for ee in (2, 1, 3):
            def to_send(lag, ee=ee):
                row = ((z_hi + ee) % 4 * 2 + lag) * BS
                return part[k, 3, pl.ds(pl.multiple_of(row, BS), BS), :]

            pack(zsums.at[k, ee - 1], 2, to_send)
            z_copy(k, ee).start()

    def finish(k):
        for ee in (1, 3, 2):
            z_copy(k, ee).wait_recv()
        for lag in range(2):
            total = part[k, 3, pl.ds(pl.multiple_of((z_hi * 2 + lag) * BS, BS), BS), :]
            for s in range(3):
                total += unpack(zgot.at[k, s], 2, lag)
            out[lag, 0, k] = (total * SCALE).astype(jnp.bfloat16)

    @pl.when(z_lo == 1)
    def _():
        step(CHUNKS)
        step(CHUNKS + 1)
        siblings_done()

    def between(q):
        for s in (0, 1):
            @pl.when(jnp.logical_and(z_lo == 0, q == s))
            def _(s=s):
                step(CHUNKS + s)

    right[...] = blocks[jnp.minimum(REACH, 15 - fibre)]
    multiply(0, between)

    @pl.when(z_lo == 0)
    def _():
        siblings_done()

    right[...] = blocks[offsets[0, 1]]
    multiply(1)
    reduce_x(0)
    right[...] = blocks[offsets[0, 2]]
    multiply(2)
    reduce_x(1)
    finish(0)
    right[...] = blocks[offsets[0, 3]]
    multiply(3)
    reduce_x(2)
    finish(1)
    reduce_x(3)
    finish(2)
    finish(3)

    @pl.when(z_lo == 1)
    def _():
        for ch in range(CHUNKS):
            far(ch).wait_send()

    for j in (1, 3):
        @pl.when(near_goes(j))
        def _(j=j):
            for ch in range(CHUNKS):
                near(j, ch).wait_send()
        for ch in range(CHUNKS):
            @pl.when(relays(j, ch))
            def _(j=j, ch=ch):
                relay(j, ch).wait_send()

    for j in range(4):
        @pl.when(chip + j + (1 - core) <= 7)
        def _(j=j):
            for ch in range(CHUNKS):
                across(j, ch).wait_send()

    for k in range(K):
        for way in (0, 1):
            middle(k, way).wait_send()
            straight(k, way).wait_send()
            summed(k, way).wait_send()
        for ee in (1, 2, 3):
            z_copy(k, ee).wait_send()


def on_device(spectra, dead_mask, partner_offset):
    vmem = pl.BlockSpec(memory_space=pltpu.VMEM)
    bf16, f32 = jnp.bfloat16, jnp.float32
    return pl.pallas_call(
        kernel,
        out_shape=jax.ShapeDtypeStruct((LAGS // BANDS, 1, K, BS, BS), bf16),
        in_specs=[vmem, vmem, pl.BlockSpec(memory_space=pltpu.SMEM), pl.BlockSpec(memory_space=pl.ANY)],
        out_specs=vmem,
        scratch_shapes=[
            pltpu.VMEM((REACH + 1, DEPTH, BS), bf16),
            pltpu.VMEM((2, BS, HALF), f32),
            pltpu.VMEM((LAGS * BS, DEPTH), bf16),
            pltpu.VMEM((DEPTH, BS), bf16),
            pltpu.VMEM((2 * LAGS, BS), f32),
            pltpu.VMEM((K, 4, XROWS, BS), f32),
            pltpu.VMEM((K, 2, 3, HX + TAIL, BS), bf16),
            pltpu.VMEM((K, 2, 3, HX + TAIL, BS), bf16),
            pltpu.VMEM((K, 3, ZROWS + TAIL, BS), bf16),
            pltpu.VMEM((K, 3, ZROWS + TAIL, BS), bf16),
            pltpu.SemaphoreType.DMA,
            pltpu.SemaphoreType.DMA((4, CHUNKS)),
            pltpu.SemaphoreType.DMA((2, CHUNKS)),
            pltpu.SemaphoreType.DMA((REACH + 1, CHUNKS)),
            pltpu.SemaphoreType.DMA((4, CHUNKS)),
            pltpu.SemaphoreType.DMA((K, 2, 3)),
            pltpu.SemaphoreType.DMA((K, 2, 3)),
            pltpu.SemaphoreType.DMA((K, 3)),
            pltpu.SemaphoreType.DMA((K, 3)),
        ],
        compiler_params=pltpu.CompilerParams(
            collective_id=0, has_side_effects=True, vmem_limit_bytes=56 * 1024 * 1024
        ),
        cost_estimate=pl.CostEstimate(
            flops=2 * LAGS * BS * DEPTH * K * BS, bytes_accessed=1 << 20, transcendentals=0
        ),
    )(spectra.reshape(DEPTH, BS), dead_mask.reshape(1, BS), partner_offset, jnp.asarray(lag_table()))


def solution(mesh):
    in_specs = (P(None, None, "band", "fibre"), P("fibre"), P("fibre", None))
    out_specs = P("band", "fibre", None, None, None)
    return jax.shard_map(
        on_device, mesh=mesh, in_specs=in_specs, out_specs=out_specs, check_vma=False
    )
```

```python
import math

import jax
import jax.numpy as jnp
import ml_dtypes
import numpy as np
from jax import lax
from jax.experimental import pallas as pl
from jax.experimental.pallas import tpu as pltpu
from jax.sharding import PartitionSpec as P

BS = 128
NF = 512
REACH = 8
K = 4
W = 32
LAGS = 32
BANDS = 16
BINS = NF // BANDS
DEPTH = 2 * W * BINS
HALF = W * BINS
CHUNKS = 4
CROWS = DEPTH // CHUNKS
XROWS = LAGS // 4 * BS
HX = XROWS // 2
ZROWS = LAGS // 16 * BS
TAIL = 16
SCALE = 1.0 / math.sqrt(W) / math.sqrt(NF)


def lag_table():
    bins = np.arange(NF)[:, None]
    lags = np.arange(LAGS)[None, :] - LAGS // 2
    angles = (bins * lags % (2 * NF)) * (math.pi / NF)
    table = np.stack([np.cos(angles), -np.sin(angles)], axis=2)
    table = table.astype(np.float32).astype(ml_dtypes.bfloat16).astype(np.float32)
    table = table.reshape(BANDS, BINS, 2 * LAGS).transpose(0, 2, 1)
    return np.tile(table, (1, 1, BS // BINS))


def kernel(
    spectra, mask, offsets, tables, out,
    blocks, spare, turned, left, right, table, part, go, come, zsums, zgot,
    table_sem, gather_send, relay_send, aside_send, around_send, around_recv, gather_recv, sib_send, x_send, x_recv, z_send, z_recv,
):
    fibre, band = lax.axis_index("fibre"), lax.axis_index("band")
    z_lo, y, core = fibre // 8, fibre // 2 % 4, fibre % 2
    chip = fibre // 2
    x, z_hi = band // 4, band % 4

    def at_fibre(zz, yy, cc):
        return {"fibre": (zz * 4 + yy) * 2 + cc, "band": band}

    def at_band(xx, zz):
        return {"fibre": fibre, "band": xx * 4 + zz}

    sibling = at_fibre(z_lo, y, 1 - core)
    other_z = at_fibre(1 - z_lo, y, core)
    y_down, y_up = at_fibre(z_lo, (y + 3) % 4, core), at_fibre(z_lo, (y + 1) % 4, core)
    x_down, x_up = at_band((x + 3) % 4, z_hi), at_band((x + 1) % 4, z_hi)
    barrier = pltpu.get_barrier_semaphore()
    peers = [sibling, other_z, y_down, y_up, x_down, x_up]
    peers += [at_band(x, (z_hi + j) % 4) for j in (1, 2, 3)]
    for peer in peers:
        pl.semaphore_signal(barrier, inc=1, device_id=peer, device_id_type=pl.DeviceIdType.MESH)

    table_copy = pltpu.make_async_copy(tables.at[band], table, table_sem)
    table_copy.start()
    alive = mask[...].astype(jnp.bfloat16)
    blocks[0] = spectra[...] * alive
    pl.semaphore_wait(barrier, len(peers))

    def remote(src, dst, send, recv, device):
        return pltpu.make_async_remote_copy(
            src_ref=src, dst_ref=dst, send_sem=send, recv_sem=recv,
            device_id=device, device_id_type=pl.DeviceIdType.MESH,
        )

    def rows_of(ch):
        return pl.ds(ch * CROWS, CROWS)

    def far(ch):
        return remote(
            blocks.at[0, rows_of(ch)], blocks.at[8, rows_of(ch)],
            gather_send.at[0, ch], gather_recv.at[8, ch], other_z,
        )

    def near(j, ch):
        src = jnp.where(y >= j, 0, 8)
        return remote(
            blocks.at[src, rows_of(ch)], blocks.at[2 * j, rows_of(ch)],
            gather_send.at[j, ch], gather_recv.at[2 * j, ch], y_down if j == 1 else y_up,
        )

    def relay(j, ch):
        return remote(
            blocks.at[2 * j, rows_of(ch)], blocks.at[4, rows_of(ch)],
            relay_send.at[j // 2, ch], gather_recv.at[4, ch], y_down if j == 1 else y_up,
        )

    def across(j, ch):
        return remote(
            blocks.at[2 * j + 2 * (1 - core), rows_of(ch)], blocks.at[2 * j + 1, rows_of(ch)],
            sib_send.at[j, ch], gather_recv.at[2 * j + 1, ch], sibling,
        )

    def aside(ch):
        return remote(
            blocks.at[0, rows_of(ch)], blocks.at[8, rows_of(ch)],
            aside_send.at[ch], gather_recv.at[8, ch], y_up,
        )

    def aside_on(ch):
        return remote(
            blocks.at[8, rows_of(ch)], blocks.at[6, rows_of(ch)],
            aside_send.at[ch], gather_recv.at[6, ch], other_z,
        )

    upper = range(CHUNKS // 2, CHUNKS)
    last_rows = rows_of(CHUNKS - 1)

    def around():
        return remote(blocks.at[0, last_rows], spare, around_send, around_recv, y_up)

    def around_on():
        return remote(spare, blocks.at[4, last_rows], around_send, gather_recv.at[4, CHUNKS - 1], y_up)

    def relays(j, ch):
        first = ch < CHUNKS // 2
        if j == 1:
            goes = y >= 1 if first else jnp.logical_and(y == 1, ch < CHUNKS - 1)
        else:
            goes = y == 2 if first else y <= 2
        return jnp.logical_and(chip + j <= 7, goes)

    def near_goes(j, ch):
        limit = 1 if j == 1 else 2 if ch in upper else 3
        return jnp.logical_or(y >= j, jnp.logical_and(z_lo == 0, y < limit))

    @pl.when(z_lo == 1)
    def _():
        for ch in range(CHUNKS):
            far(ch).start()

    for j in (1, 3):
        @pl.when(y >= j)
        def _(j=j):
            for ch in range(CHUNKS):
                near(j, ch).start()

    @pl.when(y == 2)
    def _():
        around().start()

    @pl.when(core == 1)
    def _():
        for ch in range(CHUNKS):
            across(0, ch).start()

    @pl.when(jnp.logical_and(z_lo == 1, y == 2))
    def _():
        for ch in upper:
            aside(ch).start()

    def take_far(ch):
        far(ch).wait_recv()
        for j in (1, 3):
            @pl.when(jnp.logical_and(y < j, near_goes(j, ch)))
            def _(j=j):
                near(j, ch).start()

        @pl.when(core == 0)
        def _():
            across(3, ch).start()

    def take(j, ch, when):
        @pl.when(jnp.logical_and(chip + j <= 7, when))
        def _():
            remote(
                blocks.at[0, rows_of(ch)], blocks.at[2 * j, rows_of(ch)],
                gather_send.at[0, ch], gather_recv.at[2 * j, ch], y_up,
            ).wait_recv()
            if j != 2:
                @pl.when(relays(j, ch))
                def _():
                    relay(j, ch).start()
            across(j - 1 + core, ch).start()

    def early(j, ch):
        if j == 2:
            return jnp.logical_and(z_lo == 1, y == 1)
        last = jnp.logical_or(y == 1, y == 2) if j == 1 else y == 0
        return jnp.where(z_lo == 0, relays(j, ch), last)

    def build(lag, carry):
        t0 = table[pl.ds(2 * lag, 1), :]
        t1 = table[pl.ds(2 * lag + 1, 1), :]
        rows = pl.ds(pl.multiple_of(lag * BS, BS), BS)
        for g in range(HALF // BS):
            re = turned[0, :, pl.ds(g * BS, BS)]
            im = turned[1, :, pl.ds(g * BS, BS)]
            left[rows, pl.ds(g * BS, BS)] = (t0 * re + t1 * im).astype(jnp.bfloat16)
            left[rows, pl.ds(HALF + g * BS, BS)] = (t0 * im - t1 * re).astype(jnp.bfloat16)
        return carry

    def turn(g, carry):
        rows = pl.ds(pl.multiple_of(g * BS, BS), BS)
        for r in range(2):
            turned[r, :, rows] = blocks[0, pl.ds(pl.multiple_of(r * HALF + g * BS, BS), BS), :].astype(jnp.float32).T
        return carry

    lax.fori_loop(0, HALF // BS, turn, 0)
    table_copy.wait()
    lax.fori_loop(0, LAGS // 2, build, 0)

    @pl.when(y == 3)
    def _():
        around().wait_recv()
        around_on().start()

    for s in range(CHUNKS):
        @pl.when(z_lo == 0)
        def _(s=s):
            take_far(s)
        take(1, s, early(1, s))
        if s > 0:
            take(3, s - 1, jnp.logical_and(early(3, s - 1), y != 1))
        lax.fori_loop(LAGS // 2 + s * LAGS // 8, LAGS // 2 + (s + 1) * LAGS // 8, build, 0)

    def sibling_done(j):
        for ch in range(CHUNKS):
            across(j, ch).wait_recv()

    @pl.when(z_lo == 1)
    def _():
        take(3, CHUNKS - 1, early(3, CHUNKS - 1))
        for ch in range(CHUNKS):
            take(2, ch, early(2, ch))
        for j in range(4):
            @pl.when(jnp.logical_and(core == 0, y == 3 - j))
            def _(j=j):
                sibling_done(j)

    def pass_on(ch, here):
        take(3, ch, jnp.logical_and(z_lo == 0, jnp.logical_and(relays(3, ch), here)))

    def gather_rest():
        @pl.when(jnp.logical_and(z_lo == 1, y == 3))
        def _():
            for ch in upper:
                aside(ch).wait_recv()
                aside_on(ch).start()

        for j in (1, 3, 2):
            for ch in range(CHUNKS):
                take(j, ch, jnp.logical_not(early(j, ch)))
        for j in range(4):
            taken = jnp.logical_and(z_lo == 1, jnp.logical_and(core == 0, y == 3 - j))

            @pl.when(jnp.logical_and(chip + j + core <= 7, jnp.logical_not(taken)))
            def _(j=j):
                sibling_done(j)

    def middle(k, way):
        return remote(
            go.at[k, way, 0], come.at[k, way, 0], x_send.at[k, way, 0], x_recv.at[k, way, 0],
            x_down if way else x_up,
        )

    def straight(k, way):
        return remote(
            go.at[k, way, 1], come.at[k, way, 1], x_send.at[k, way, 1], x_recv.at[k, way, 1],
            x_down if way else x_up,
        )

    def summed(k, way):
        return remote(
            go.at[k, way, 2], come.at[k, way, 2], x_send.at[k, way, 2], x_recv.at[k, way, 2],
            x_down if way else x_up,
        )

    def z_copy(k, ee):
        return remote(
            zsums.at[k, ee - 1], zgot.at[k, ee - 1], z_send.at[k, ee - 1], z_recv.at[k, ee - 1],
            at_band(x, (z_hi + ee) % 4),
        )

    square = (BS, BS)
    diagonal = lax.broadcasted_iota(jnp.int32, square, 0) == lax.broadcasted_iota(jnp.int32, square, 1)
    tail_row = lax.broadcasted_iota(jnp.int32, (TAIL, BS), 0)

    def pack(message, lags, value_of):
        tail = jnp.zeros((TAIL, BS), jnp.float32)
        for lag in range(lags):
            value = value_of(lag)
            rounded = value.astype(jnp.bfloat16)
            message[pl.ds(lag * BS, BS), :] = rounded
            rest = jnp.where(diagonal, value - rounded.astype(jnp.float32), 0.0)
            tail = jnp.where(tail_row == lag, jnp.sum(rest, axis=0, keepdims=True), tail)
        message[pl.ds(lags * BS, TAIL), :] = tail.astype(jnp.bfloat16)

    def unpack(message, lags, lag):
        tail = message[pl.ds(lags * BS, TAIL), :].astype(jnp.float32)[lag:lag + 1]
        return message[pl.ds(lag * BS, BS), :].astype(jnp.float32) + jnp.where(diagonal, tail, 0.0)

    def part_of(k, q, lag):
        return part[k, q, pl.ds(lag * BS, BS), :]

    def send_middle(k):
        for way in (0, 1):
            pack(go.at[k, way, 0], 4, lambda lag, way=way: part_of(k, 0, way * 4 + lag))
            middle(k, way).start()

    def send_straight(k, way):
        pack(go.at[k, way, 1], 4, lambda lag: part_of(k, 1 + way, (1 - way) * 4 + lag))
        straight(k, way).start()

    def send_summed(k):
        for way in (0, 1):
            def both(lag, way=way):
                return part_of(k, 1 + way, way * 4 + lag) + unpack(come.at[k, way, 0], 4, lag)

            middle(k, way).wait_recv()
            pack(go.at[k, way, 2], 4, both)
            summed(k, way).start()

    def multiply(slots, *after):
        width = len(slots) * BS

        def quarter(q, carry):
            ahead = jnp.where(q == 0, 2, jnp.where(q == 1, 1, jnp.where(q == 2, 3, 0)))
            rows = pl.ds(pl.multiple_of((x + ahead) % 4 * XROWS, XROWS), XROWS)
            total = jnp.dot(left[rows, :], right[:, pl.ds(0, width)], preferred_element_type=jnp.float32)
            for n, k in enumerate(slots):
                part[k, q] = total[:, n * BS:(n + 1) * BS]
            for at, then in enumerate(after):
                pl.when(q == at)(then)
            return carry

        lax.fori_loop(0, 4, quarter, 0)

    def reduce_x(k):
        for way in (0, 1):
            straight(k, way).wait_recv()
            summed(k, way).wait_recv()
        for lag in range(8):
            up = 2 if lag < 4 else 1
            total = part_of(k, 3, lag) + unpack(come.at[k, 0, up], 4, lag % 4)
            part[k, 3, pl.ds(lag * BS, BS), :] = total + unpack(come.at[k, 1, 3 - up], 4, lag % 4)
        for ee in (2, 1, 3):
            def to_send(lag, ee=ee):
                row = ((z_hi + ee) % 4 * 2 + lag) * BS
                return part[k, 3, pl.ds(pl.multiple_of(row, BS), BS), :]

            pack(zsums.at[k, ee - 1], 2, to_send)
            z_copy(k, ee).start()

    def finish(k):
        for ee in (1, 3, 2):
            z_copy(k, ee).wait_recv()
        for lag in range(2):
            total = part[k, 3, pl.ds(pl.multiple_of((z_hi * 2 + lag) * BS, BS), BS), :]
            for s in range(3):
                total += unpack(zgot.at[k, s], 2, lag)
            out[lag, 0, k] = (total * SCALE).astype(jnp.bfloat16)

    right[:, pl.ds(0, BS)] = blocks[jnp.minimum(REACH, 15 - fibre)]
    def zero_0():
        send_middle(0)
        pass_on(3, y != 1)
        pass_on(2, y == 1)

    def zero_1():
        send_straight(0, 0)
        pass_on(3, y == 1)

    multiply((0,), zero_0, zero_1, lambda: send_straight(0, 1), lambda: send_summed(0))
    gather_rest()
    for n, slot in enumerate((1, 2)):
        right[:, pl.ds(n * BS, BS)] = blocks[offsets[0, slot]]

    def two_3():
        send_middle(2)
        send_summed(1)
        send_straight(2, 0)
        send_straight(2, 1)
        reduce_x(0)

    multiply((1, 2), lambda: send_middle(1), lambda: send_straight(1, 0), lambda: send_straight(1, 1), two_3)
    right[:, pl.ds(0, BS)] = blocks[offsets[0, 3]]

    def three_0():
        send_middle(3)
        send_summed(2)

    def three_3():
        finish(0)
        reduce_x(1)
        send_summed(3)

    multiply((3,), three_0, lambda: send_straight(3, 0), lambda: send_straight(3, 1), three_3)
    reduce_x(2)
    finish(1)
    reduce_x(3)
    finish(2)
    finish(3)

    @pl.when(y >= 2)
    def _():
        around().wait_send()

    @pl.when(jnp.logical_and(z_lo == 1, y >= 2))
    def _():
        for ch in upper:
            aside(ch).wait_send()

    @pl.when(z_lo == 1)
    def _():
        for ch in range(CHUNKS):
            far(ch).wait_send()

    for j in (1, 3):
        for ch in range(CHUNKS):
            @pl.when(near_goes(j, ch))
            def _(j=j, ch=ch):
                near(j, ch).wait_send()

            @pl.when(relays(j, ch))
            def _(j=j, ch=ch):
                relay(j, ch).wait_send()

    for j in range(4):
        @pl.when(chip + j + (1 - core) <= 7)
        def _(j=j):
            for ch in range(CHUNKS):
                across(j, ch).wait_send()

    for k in range(K):
        for way in (0, 1):
            middle(k, way).wait_send()
            straight(k, way).wait_send()
            summed(k, way).wait_send()
        for ee in (1, 2, 3):
            z_copy(k, ee).wait_send()


def on_device(spectra, dead_mask, partner_offset):
    vmem = pl.BlockSpec(memory_space=pltpu.VMEM)
    bf16, f32 = jnp.bfloat16, jnp.float32
    return pl.pallas_call(
        kernel,
        out_shape=jax.ShapeDtypeStruct((LAGS // BANDS, 1, K, BS, BS), bf16),
        in_specs=[vmem, vmem, pl.BlockSpec(memory_space=pltpu.SMEM), pl.BlockSpec(memory_space=pl.ANY)],
        out_specs=vmem,
        scratch_shapes=[
            pltpu.VMEM((REACH + 1, DEPTH, BS), bf16),
            pltpu.VMEM((CROWS, BS), bf16),
            pltpu.VMEM((2, BS, HALF), f32),
            pltpu.VMEM((LAGS * BS, DEPTH), bf16),
            pltpu.VMEM((DEPTH, 2 * BS), bf16),
            pltpu.VMEM((2 * LAGS, BS), f32),
            pltpu.VMEM((K, 4, XROWS, BS), f32),
            pltpu.VMEM((K, 2, 3, HX + TAIL, BS), bf16),
            pltpu.VMEM((K, 2, 3, HX + TAIL, BS), bf16),
            pltpu.VMEM((K, 3, ZROWS + TAIL, BS), bf16),
            pltpu.VMEM((K, 3, ZROWS + TAIL, BS), bf16),
            pltpu.SemaphoreType.DMA,
            pltpu.SemaphoreType.DMA((4, CHUNKS)),
            pltpu.SemaphoreType.DMA((2, CHUNKS)),
            pltpu.SemaphoreType.DMA((CHUNKS,)),
            pltpu.SemaphoreType.DMA,
            pltpu.SemaphoreType.DMA,
            pltpu.SemaphoreType.DMA((REACH + 1, CHUNKS)),
            pltpu.SemaphoreType.DMA((4, CHUNKS)),
            pltpu.SemaphoreType.DMA((K, 2, 3)),
            pltpu.SemaphoreType.DMA((K, 2, 3)),
            pltpu.SemaphoreType.DMA((K, 3)),
            pltpu.SemaphoreType.DMA((K, 3)),
        ],
        compiler_params=pltpu.CompilerParams(
            collective_id=0, has_side_effects=True, vmem_limit_bytes=56 * 1024 * 1024
        ),
        cost_estimate=pl.CostEstimate(
            flops=2 * LAGS * BS * DEPTH * K * BS, bytes_accessed=1 << 20, transcendentals=0
        ),
    )(spectra.reshape(DEPTH, BS), dead_mask.reshape(1, BS), partner_offset, jnp.asarray(lag_table()))


def solution(mesh):
    in_specs = (P(None, None, "band", "fibre"), P("fibre"), P("fibre", None))
    out_specs = P("band", "fibre", None, None, None)
    return jax.shard_map(
        on_device, mesh=mesh, in_specs=in_specs, out_specs=out_specs, check_vma=False
    )
```

```python
import math

import jax
import jax.numpy as jnp
import ml_dtypes
import numpy as np
from jax import lax
from jax.experimental import pallas as pl
from jax.experimental.pallas import tpu as pltpu
from jax.sharding import PartitionSpec as P

BS = 128
NF = 512
REACH = 8
K = 4
W = 32
LAGS = 32
BANDS = 16
BINS = NF // BANDS
DEPTH = 2 * W * BINS
HALF = W * BINS
CHUNKS = 4
CROWS = DEPTH // CHUNKS
XROWS = LAGS // 4 * BS
HX = XROWS // 2
ZROWS = LAGS // 16 * BS
TAIL = 16
SCALE = 1.0 / math.sqrt(W) / math.sqrt(NF)


def lag_table():
    bins = np.arange(NF)[:, None]
    lags = np.arange(LAGS)[None, :] - LAGS // 2
    angles = (bins * lags % (2 * NF)) * (math.pi / NF)
    table = np.stack([np.cos(angles), -np.sin(angles)], axis=2)
    table = table.astype(np.float32).astype(ml_dtypes.bfloat16).astype(np.float32)
    table = table.reshape(BANDS, BINS, 2 * LAGS).transpose(0, 2, 1)
    return np.tile(table, (1, 1, BS // BINS))


def kernel(
    spectra, mask, offsets, tables, out,
    blocks, spare, turned, left, right, table, part, go, come, zsums, zgot,
    table_sem, gather_send, relay_send, aside_send, around_send, around_recv, gather_recv, sib_send, x_send, x_recv, z_send, z_recv,
):
    fibre, band = lax.axis_index("fibre"), lax.axis_index("band")
    z_lo, y, core = fibre // 8, fibre // 2 % 4, fibre % 2
    chip = fibre // 2
    x, z_hi = band // 4, band % 4

    def at_fibre(zz, yy, cc):
        return {"fibre": (zz * 4 + yy) * 2 + cc, "band": band}

    def at_band(xx, zz):
        return {"fibre": fibre, "band": xx * 4 + zz}

    sibling = at_fibre(z_lo, y, 1 - core)
    other_z = at_fibre(1 - z_lo, y, core)
    y_down, y_up = at_fibre(z_lo, (y + 3) % 4, core), at_fibre(z_lo, (y + 1) % 4, core)
    x_down, x_up = at_band((x + 3) % 4, z_hi), at_band((x + 1) % 4, z_hi)
    barrier = pltpu.get_barrier_semaphore()
    peers = [sibling, other_z, y_down, y_up, x_down, x_up]
    peers += [at_band(x, (z_hi + j) % 4) for j in (1, 2, 3)]
    for peer in peers:
        pl.semaphore_signal(barrier, inc=1, device_id=peer, device_id_type=pl.DeviceIdType.MESH)

    table_copy = pltpu.make_async_copy(tables.at[band], table, table_sem)
    table_copy.start()
    alive = mask[...].astype(jnp.bfloat16)
    blocks[0] = spectra[...] * alive
    pl.semaphore_wait(barrier, len(peers))

    def remote(src, dst, send, recv, device):
        return pltpu.make_async_remote_copy(
            src_ref=src, dst_ref=dst, send_sem=send, recv_sem=recv,
            device_id=device, device_id_type=pl.DeviceIdType.MESH,
        )

    def rows_of(ch):
        return pl.ds(ch * CROWS, CROWS)

    def far(ch):
        return remote(
            blocks.at[0, rows_of(ch)], blocks.at[8, rows_of(ch)],
            gather_send.at[0, ch], gather_recv.at[8, ch], other_z,
        )

    def near(j, ch):
        src = jnp.where(y >= j, 0, 8)
        return remote(
            blocks.at[src, rows_of(ch)], blocks.at[2 * j, rows_of(ch)],
            gather_send.at[j, ch], gather_recv.at[2 * j, ch], y_down if j == 1 else y_up,
        )

    def relay(j, ch):
        return remote(
            blocks.at[2 * j, rows_of(ch)], blocks.at[4, rows_of(ch)],
            relay_send.at[j // 2, ch], gather_recv.at[4, ch], y_down if j == 1 else y_up,
        )

    def across(j, ch):
        return remote(
            blocks.at[2 * j + 2 * (1 - core), rows_of(ch)], blocks.at[2 * j + 1, rows_of(ch)],
            sib_send.at[j, ch], gather_recv.at[2 * j + 1, ch], sibling,
        )

    def aside(ch):
        return remote(
            blocks.at[0, rows_of(ch)], blocks.at[8, rows_of(ch)],
            aside_send.at[ch], gather_recv.at[8, ch], y_up,
        )

    def aside_on(ch):
        return remote(
            blocks.at[8, rows_of(ch)], blocks.at[6, rows_of(ch)],
            aside_send.at[ch], gather_recv.at[6, ch], other_z,
        )

    upper = range(CHUNKS // 2, CHUNKS)
    last_rows = rows_of(CHUNKS - 1)

    def around():
        return remote(blocks.at[0, last_rows], spare, around_send, around_recv, y_up)

    def around_on():
        return remote(spare, blocks.at[4, last_rows], around_send, gather_recv.at[4, CHUNKS - 1], y_up)

    def relays(j, ch):
        first = ch < CHUNKS // 2
        if j == 1:
            goes = y >= 1 if first else jnp.logical_and(y == 1, ch < CHUNKS - 1)
        else:
            goes = y == 2 if first else y <= 2
        return jnp.logical_and(chip + j <= 7, goes)

    def near_goes(j, ch):
        limit = 1 if j == 1 else 2 if ch in upper else 3
        return jnp.logical_or(y >= j, jnp.logical_and(z_lo == 0, y < limit))

    @pl.when(z_lo == 1)
    def _():
        for ch in range(CHUNKS):
            far(ch).start()

    own_turn = [*upper, *range(CHUNKS // 2)]
    held = jnp.logical_and(z_lo == 1, y == 2)
    waits = jnp.logical_and(z_lo == 1, y == 1)

    @pl.when(y >= 1)
    def _():
        for ch in range(CHUNKS // 2):
            near(1, ch).start()

    @pl.when(jnp.logical_and(y >= 1, jnp.logical_not(held)))
    def _():
        for ch in upper:
            near(1, ch).start()

    @pl.when(y == 3)
    def _():
        for ch in own_turn:
            near(3, ch).start()

    @pl.when(y == 2)
    def _():
        around().start()

    @pl.when(core == 1)
    def _():
        for ch in range(CHUNKS):
            across(0, ch).start()

    @pl.when(jnp.logical_and(z_lo == 1, y == 2))
    def _():
        for ch in upper:
            aside(ch).start()

    def take_far(ch):
        far(ch).wait_recv()
        for j in (1, 3):
            @pl.when(jnp.logical_and(y < j, near_goes(j, ch)))
            def _(j=j):
                near(j, ch).start()

        @pl.when(core == 0)
        def _():
            across(3, ch).start()

    def take(j, ch, when):
        @pl.when(jnp.logical_and(chip + j <= 7, when))
        def _():
            remote(
                blocks.at[0, rows_of(ch)], blocks.at[2 * j, rows_of(ch)],
                gather_send.at[0, ch], gather_recv.at[2 * j, ch], y_up,
            ).wait_recv()
            if j != 2:
                @pl.when(relays(j, ch))
                def _():
                    relay(j, ch).start()
            across(j - 1 + core, ch).start()

    def early(j, ch):
        if j == 2:
            return jnp.logical_and(z_lo == 1, y == 1)
        last = jnp.logical_or(y == 1, y == 2) if j == 1 else y == 0
        return jnp.where(z_lo == 0, relays(j, ch), last)

    def build(lag, carry):
        t0 = table[pl.ds(2 * lag, 1), :]
        t1 = table[pl.ds(2 * lag + 1, 1), :]
        rows = pl.ds(pl.multiple_of(lag * BS, BS), BS)
        for g in range(HALF // BS):
            re = turned[0, :, pl.ds(g * BS, BS)]
            im = turned[1, :, pl.ds(g * BS, BS)]
            left[rows, pl.ds(g * BS, BS)] = (t0 * re + t1 * im).astype(jnp.bfloat16)
            left[rows, pl.ds(HALF + g * BS, BS)] = (t0 * im - t1 * re).astype(jnp.bfloat16)
        return carry

    def turn(g, carry):
        rows = pl.ds(pl.multiple_of(g * BS, BS), BS)
        for r in range(2):
            turned[r, :, rows] = blocks[0, pl.ds(pl.multiple_of(r * HALF + g * BS, BS), BS), :].astype(jnp.float32).T
        return carry

    lax.fori_loop(0, HALF // BS, turn, 0)
    table_copy.wait()
    lax.fori_loop(0, LAGS // 2, build, 0)

    @pl.when(y == 3)
    def _():
        around().wait_recv()
        around_on().start()

    for s in range(CHUNKS):
        @pl.when(z_lo == 0)
        def _(s=s):
            take_far(s)
        take(1, s, early(1, s) if s < CHUNKS // 2 else jnp.logical_and(early(1, s), jnp.logical_not(waits)))
        take(3, own_turn[s], jnp.logical_and(z_lo == 1, early(3, own_turn[s])))
        if s > 0:
            take(3, s - 1, jnp.logical_and(z_lo == 0, jnp.logical_and(relays(3, s - 1), y != 1)))
        if s == CHUNKS // 2 - 1:
            @pl.when(held)
            def _():
                for ch in upper:
                    near(1, ch).start()
        lax.fori_loop(LAGS // 2 + s * LAGS // 8, LAGS // 2 + (s + 1) * LAGS // 8, build, 0)

    def sibling_done(j):
        for ch in range(CHUNKS):
            across(j, ch).wait_recv()

    @pl.when(z_lo == 1)
    def _():
        for ch in range(CHUNKS):
            take(2, ch, early(2, ch))
        for j in range(4):
            @pl.when(jnp.logical_and(core == 0, y == 3 - j))
            def _(j=j):
                sibling_done(j)

    def pass_on(ch, yy):
        take(3, ch, jnp.logical_and(z_lo == 0, y == yy))

    def take_late(j, ch):
        take(j, ch, jnp.logical_not(early(j, ch)))

    def gather_rest():
        @pl.when(jnp.logical_and(z_lo == 1, y == 3))
        def _():
            for ch in upper:
                aside(ch).wait_recv()
                aside_on(ch).start()

        for j in (3, 2):
            for ch in upper:
                take_late(j, ch)
        for j in range(4):
            taken = jnp.logical_and(z_lo == 1, jnp.logical_and(core == 0, y == 3 - j))

            @pl.when(jnp.logical_and(chip + j + core <= 7, jnp.logical_not(taken)))
            def _(j=j):
                sibling_done(j)

    def pieces_of(k):
        return 2 if k == K - 1 else 1

    def hop(k, way, kind):
        used = pl.ds(0, HX)
        if kind >= 2:
            size = HX // pieces_of(k) + TAIL
            used = pl.ds((kind - 2) * size, size)
        place = min(kind, 2)
        return remote(
            go.at[k, way, place, used], come.at[k, way, place, used],
            x_send.at[k, way, kind], x_recv.at[k, way, kind], x_down if way else x_up,
        )

    def z_copy(k, ee):
        return remote(
            zsums.at[k, ee - 1], zgot.at[k, ee - 1], z_send.at[k, ee - 1], z_recv.at[k, ee - 1],
            at_band(x, (z_hi + ee) % 4),
        )

    square = (BS, BS)
    diagonal = lax.broadcasted_iota(jnp.int32, square, 0) == lax.broadcasted_iota(jnp.int32, square, 1)
    tail_row = lax.broadcasted_iota(jnp.int32, (TAIL, BS), 0)

    def pack(message, lags, value_of):
        tail = jnp.zeros((TAIL, BS), jnp.float32)
        for lag in range(lags):
            value = value_of(lag)
            rounded = value.astype(jnp.bfloat16)
            message[pl.ds(lag * BS, BS), :] = rounded
            rest = jnp.where(diagonal, value - rounded.astype(jnp.float32), 0.0)
            tail = jnp.where(tail_row == lag, jnp.sum(rest, axis=0, keepdims=True), tail)
        message[pl.ds(lags * BS, TAIL), :] = tail.astype(jnp.bfloat16)

    def plain(message, value_of):
        for lag in range(4):
            message[pl.ds(lag * BS, BS), :] = value_of(lag).astype(jnp.bfloat16)

    def unpack(message, lags, lag):
        tail = message[pl.ds(lags * BS, TAIL), :].astype(jnp.float32)[lag:lag + 1]
        return message[pl.ds(lag * BS, BS), :].astype(jnp.float32) + jnp.where(diagonal, tail, 0.0)

    def rows_at(place):
        return pl.ds(pl.multiple_of(place * BS, BS), BS)

    def send_middle(k, way):
        plain(go.at[k, way, 0], lambda lag: part[k, 0, rows_at(way * 4 + lag), :])
        hop(k, way, 0).start()

    def send_straight(k, way):
        plain(go.at[k, way, 1], lambda lag: part[k, 1 + way, rows_at((1 - way) * 4 + lag), :])
        hop(k, way, 1).start()

    def send_summed(k):
        count = 4 // pieces_of(k)
        size = HX // pieces_of(k) + TAIL
        for piece in range(pieces_of(k)):
            for way in (0, 1):
                def both(lag, way=way, at=piece * count):
                    through = come[k, way, 0, rows_at(at + lag), :].astype(jnp.float32)
                    return part[k, 1 + way, rows_at(way * 4 + at + lag), :] + through

                if piece == 0:
                    hop(k, way, 0).wait_recv()
                pack(go.at[k, way, 2, pl.ds(piece * size, size)], count, both)
                hop(k, way, 2 + piece).start()

    def reduce_x(k):
        count = 4 // pieces_of(k)
        size = HX // pieces_of(k) + TAIL
        for way in (0, 1):
            hop(k, way, 1).wait_recv()
        for piece in range(pieces_of(k)):
            for way in (0, 1):
                hop(k, way, 2 + piece).wait_recv()
                for lag in range(count):
                    at = piece * count + lag
                    rows = rows_at(way * 4 + at)
                    straight = come[k, 1 - way, 1, rows_at(at), :].astype(jnp.float32)
                    summed = unpack(come.at[k, way, 2, pl.ds(piece * size, size)], count, lag)
                    part[k, 3, rows, :] = part[k, 3, rows, :] + straight + summed
            if pieces_of(k) == 1:
                for ee in (2, 1, 3):
                    send_z(k, ee)
            else:
                for e in (piece, 2 + piece):
                    @pl.when(e != z_hi)
                    def _(e=e):
                        send_z(k, (e + 4 - z_hi) % 4)

    def send_z(k, ee):
        e = (z_hi + ee) % 4
        pack(zsums.at[k, ee - 1], 2, lambda lag: part[k, 3, rows_at(e * 2 + lag), :])
        z_copy(k, ee).start()

    def finish(k):
        for ee in (1, 3, 2):
            z_copy(k, ee).wait_recv()
        for lag in range(2):
            total = part[k, 3, rows_at(z_hi * 2 + lag), :]
            for s in range(3):
                total += unpack(zgot.at[k, s], 2, lag)
            out[lag, 0, k] = (total * SCALE).astype(jnp.bfloat16)

    def pick(t, values):
        chosen = jnp.int32(values[-1])
        for at in range(len(values) - 1):
            chosen = jnp.where(t == at, values[at], chosen)
        return chosen

    def multiply(slots, *after):
        width = len(slots) * BS

        def step(t, carry):
            q = pick(t, (0, 0, 1, 2, 1, 2, 3, 3))
            high = pick(t, (0, 1, 1, 0, 0, 1, 0, 1))
            ahead = pick(t, (2, 2, 1, 3, 1, 3, 0, 0))
            rows = pl.ds(pl.multiple_of(((x + ahead) % 4 * 2 + high) * HX, HX), HX)
            total = jnp.dot(left[rows, :], right[:, pl.ds(0, width)], preferred_element_type=jnp.float32)
            for n, k in enumerate(slots):
                part[k, q, pl.ds(pl.multiple_of(high * HX, HX), HX), :] = total[:, n * BS:(n + 1) * BS]
            for at, then in enumerate(after):
                pl.when(t == at)(then)
            return carry

        lax.fori_loop(0, 8, step, 0)

    def run(*steps):
        def then():
            for step in steps:
                step[0](*step[1:])

        return then

    right[:, pl.ds(0, BS)] = blocks[jnp.minimum(REACH, 15 - fibre)]
    multiply(
        (0,),
        run((send_middle, 0, 0), (pass_on, 3, 0)),
        run((send_middle, 0, 1), (pass_on, 2, 1), (pass_on, 3, 2), (take, 1, 2, waits)),
        run((send_straight, 0, 0)),
        run((send_straight, 0, 1), (pass_on, 3, 1), (take, 1, 3, waits)),
        run(),
        run((take_late, 3, 0), (take_late, 3, 1)),
        run(*((take_late, 1, ch) for ch in range(CHUNKS))),
        run((send_summed, 0), (take_late, 2, 0), (take_late, 2, 1)),
    )
    gather_rest()
    for n, slot in enumerate((1, 2)):
        right[:, pl.ds(n * BS, BS)] = blocks[offsets[0, slot]]
    multiply(
        (1, 2),
        run((send_middle, 1, 0)),
        run((send_middle, 1, 1)),
        run((send_straight, 1, 0)),
        run((send_straight, 1, 1)),
        run((send_middle, 2, 0), (send_middle, 2, 1)),
        run(),
        run((send_summed, 1)),
        run((send_straight, 2, 0), (send_straight, 2, 1), (reduce_x, 0)),
    )
    right[:, pl.ds(0, BS)] = blocks[offsets[0, 3]]
    multiply(
        (3,),
        run((send_middle, 3, 0)),
        run((send_middle, 3, 1), (send_summed, 2)),
        run((send_straight, 3, 0)),
        run((send_straight, 3, 1), (finish, 0), (reduce_x, 1)),
        run(),
        run(),
        run(),
        run((send_summed, 3)),
    )
    reduce_x(2)
    finish(1)
    reduce_x(3)
    finish(2)
    finish(3)

    @pl.when(y >= 2)
    def _():
        around().wait_send()

    @pl.when(jnp.logical_and(z_lo == 1, y >= 2))
    def _():
        for ch in upper:
            aside(ch).wait_send()

    @pl.when(z_lo == 1)
    def _():
        for ch in range(CHUNKS):
            far(ch).wait_send()

    for j in (1, 3):
        for ch in range(CHUNKS):
            @pl.when(near_goes(j, ch))
            def _(j=j, ch=ch):
                near(j, ch).wait_send()

            @pl.when(relays(j, ch))
            def _(j=j, ch=ch):
                relay(j, ch).wait_send()

    for j in range(4):
        @pl.when(chip + j + (1 - core) <= 7)
        def _(j=j):
            for ch in range(CHUNKS):
                across(j, ch).wait_send()

    for k in range(K):
        for way in (0, 1):
            for kind in range(2 + pieces_of(k)):
                hop(k, way, kind).wait_send()
        for ee in (1, 2, 3):
            z_copy(k, ee).wait_send()


def on_device(spectra, dead_mask, partner_offset):
    vmem = pl.BlockSpec(memory_space=pltpu.VMEM)
    bf16, f32 = jnp.bfloat16, jnp.float32
    return pl.pallas_call(
        kernel,
        out_shape=jax.ShapeDtypeStruct((LAGS // BANDS, 1, K, BS, BS), bf16),
        in_specs=[vmem, vmem, pl.BlockSpec(memory_space=pltpu.SMEM), pl.BlockSpec(memory_space=pl.ANY)],
        out_specs=vmem,
        scratch_shapes=[
            pltpu.VMEM((REACH + 1, DEPTH, BS), bf16),
            pltpu.VMEM((CROWS, BS), bf16),
            pltpu.VMEM((2, BS, HALF), f32),
            pltpu.VMEM((LAGS * BS, DEPTH), bf16),
            pltpu.VMEM((DEPTH, 2 * BS), bf16),
            pltpu.VMEM((2 * LAGS, BS), f32),
            pltpu.VMEM((K, 4, XROWS, BS), f32),
            pltpu.VMEM((K, 2, 3, HX + 2 * TAIL, BS), bf16),
            pltpu.VMEM((K, 2, 3, HX + 2 * TAIL, BS), bf16),
            pltpu.VMEM((K, 3, ZROWS + TAIL, BS), bf16),
            pltpu.VMEM((K, 3, ZROWS + TAIL, BS), bf16),
            pltpu.SemaphoreType.DMA,
            pltpu.SemaphoreType.DMA((4, CHUNKS)),
            pltpu.SemaphoreType.DMA((2, CHUNKS)),
            pltpu.SemaphoreType.DMA((CHUNKS,)),
            pltpu.SemaphoreType.DMA,
            pltpu.SemaphoreType.DMA,
            pltpu.SemaphoreType.DMA((REACH + 1, CHUNKS)),
            pltpu.SemaphoreType.DMA((4, CHUNKS)),
            pltpu.SemaphoreType.DMA((K, 2, 4)),
            pltpu.SemaphoreType.DMA((K, 2, 4)),
            pltpu.SemaphoreType.DMA((K, 3)),
            pltpu.SemaphoreType.DMA((K, 3)),
        ],
        compiler_params=pltpu.CompilerParams(
            collective_id=0, has_side_effects=True, vmem_limit_bytes=56 * 1024 * 1024
        ),
        cost_estimate=pl.CostEstimate(
            flops=2 * LAGS * BS * DEPTH * K * BS, bytes_accessed=1 << 20, transcendentals=0
        ),
    )(spectra.reshape(DEPTH, BS), dead_mask.reshape(1, BS), partner_offset, jnp.asarray(lag_table()))


def solution(mesh):
    in_specs = (P(None, None, "band", "fibre"), P("fibre"), P("fibre", None))
    out_specs = P("band", "fibre", None, None, None)
    return jax.shard_map(
        on_device, mesh=mesh, in_specs=in_specs, out_specs=out_specs, check_vma=False
    )
```

```python
import math

import jax
import jax.numpy as jnp
import ml_dtypes
import numpy as np
from jax import lax
from jax.experimental import pallas as pl
from jax.experimental.pallas import tpu as pltpu
from jax.sharding import PartitionSpec as P

BS = 128
NF = 512
REACH = 8
K = 4
W = 32
LAGS = 32
BANDS = 16
BINS = NF // BANDS
DEPTH = 2 * W * BINS
HALF = W * BINS
CHUNKS = 4
CROWS = DEPTH // CHUNKS
XROWS = LAGS // 4 * BS
HX = XROWS // 2
ZROWS = LAGS // 16 * BS
TAIL = 16
SCALE = 1.0 / math.sqrt(W) / math.sqrt(NF)


def lag_table():
    bins = np.arange(NF)[:, None]
    lags = np.arange(LAGS)[None, :] - LAGS // 2
    angles = (bins * lags % (2 * NF)) * (math.pi / NF)
    table = np.stack([np.cos(angles), -np.sin(angles)], axis=2)
    table = table.astype(np.float32).astype(ml_dtypes.bfloat16).astype(np.float32)
    table = table.reshape(BANDS, BINS, 2 * LAGS).transpose(0, 2, 1)
    return np.tile(table, (1, 1, BS // BINS))


def kernel(
    spectra, mask, offsets, tables, out,
    raw, done, raw_sem, done_sem, blocks, spare, turned, left, right, table, part, go, come, zsums, zgot,
    table_sem, gather_send, relay_send, aside_send, around_send, around_recv, gather_recv, sib_send, x_send, x_recv, z_send, z_recv,
):
    fibre, band = lax.axis_index("fibre"), lax.axis_index("band")
    z_lo, y, core = fibre // 8, fibre // 2 % 4, fibre % 2
    chip = fibre // 2
    x, z_hi = band // 4, band % 4

    def at_fibre(zz, yy, cc):
        return {"fibre": (zz * 4 + yy) * 2 + cc, "band": band}

    def at_band(xx, zz):
        return {"fibre": fibre, "band": xx * 4 + zz}

    sibling = at_fibre(z_lo, y, 1 - core)
    other_z = at_fibre(1 - z_lo, y, core)
    y_down, y_up = at_fibre(z_lo, (y + 3) % 4, core), at_fibre(z_lo, (y + 1) % 4, core)
    x_down, x_up = at_band((x + 3) % 4, z_hi), at_band((x + 1) % 4, z_hi)
    raw_copy = pltpu.make_async_copy(spectra, raw, raw_sem)
    raw_copy.start()
    barrier = pltpu.get_barrier_semaphore()
    peers = [sibling, other_z, y_down, y_up, x_down, x_up]
    peers += [at_band(x, (z_hi + j) % 4) for j in (1, 2, 3)]
    for peer in peers:
        pl.semaphore_signal(barrier, inc=1, device_id=peer, device_id_type=pl.DeviceIdType.MESH)

    table_copy = pltpu.make_async_copy(tables.at[band], table, table_sem)
    table_copy.start()
    alive = mask[...].astype(jnp.bfloat16)
    raw_copy.wait()
    blocks[0] = raw[...] * alive
    pl.semaphore_wait(barrier, len(peers))

    def remote(src, dst, send, recv, device):
        return pltpu.make_async_remote_copy(
            src_ref=src, dst_ref=dst, send_sem=send, recv_sem=recv,
            device_id=device, device_id_type=pl.DeviceIdType.MESH,
        )

    def rows_of(ch):
        return pl.ds(ch * CROWS, CROWS)

    def far(ch):
        return remote(
            blocks.at[0, rows_of(ch)], blocks.at[8, rows_of(ch)],
            gather_send.at[0, ch], gather_recv.at[8, ch], other_z,
        )

    def near(j, ch):
        src = jnp.where(y >= j, 0, 8)
        return remote(
            blocks.at[src, rows_of(ch)], blocks.at[2 * j, rows_of(ch)],
            gather_send.at[j, ch], gather_recv.at[2 * j, ch], y_down if j == 1 else y_up,
        )

    def relay(j, ch):
        return remote(
            blocks.at[2 * j, rows_of(ch)], blocks.at[4, rows_of(ch)],
            relay_send.at[j // 2, ch], gather_recv.at[4, ch], y_down if j == 1 else y_up,
        )

    def across(j, ch):
        return remote(
            blocks.at[2 * j + 2 * (1 - core), rows_of(ch)], blocks.at[2 * j + 1, rows_of(ch)],
            sib_send.at[j, ch], gather_recv.at[2 * j + 1, ch], sibling,
        )

    def aside(ch):
        return remote(
            blocks.at[0, rows_of(ch)], blocks.at[8, rows_of(ch)],
            aside_send.at[ch], gather_recv.at[8, ch], y_up,
        )

    def aside_on(ch):
        return remote(
            blocks.at[8, rows_of(ch)], blocks.at[6, rows_of(ch)],
            aside_send.at[ch], gather_recv.at[6, ch], other_z,
        )

    upper = range(CHUNKS // 2, CHUNKS)
    last_rows = rows_of(CHUNKS - 1)

    def around():
        return remote(blocks.at[0, last_rows], spare, around_send, around_recv, y_up)

    def around_on():
        return remote(spare, blocks.at[4, last_rows], around_send, gather_recv.at[4, CHUNKS - 1], y_up)

    def relays(j, ch):
        first = ch < CHUNKS // 2
        if j == 1:
            goes = y >= 1 if first else jnp.logical_and(y == 1, ch < CHUNKS - 1)
        else:
            goes = y == 2 if first else y <= 2
        return jnp.logical_and(chip + j <= 7, goes)

    def near_goes(j, ch):
        limit = 1 if j == 1 else 2 if ch in upper else 3
        return jnp.logical_or(y >= j, jnp.logical_and(z_lo == 0, y < limit))

    @pl.when(z_lo == 1)
    def _():
        for ch in range(CHUNKS):
            far(ch).start()

    own_turn = [*upper, *range(CHUNKS // 2)]
    held = jnp.logical_and(z_lo == 1, y == 2)
    waits = jnp.logical_and(z_lo == 1, y == 1)

    @pl.when(y >= 1)
    def _():
        for ch in range(CHUNKS // 2):
            near(1, ch).start()

    @pl.when(jnp.logical_and(y >= 1, jnp.logical_not(held)))
    def _():
        for ch in upper:
            near(1, ch).start()

    @pl.when(y == 3)
    def _():
        for ch in own_turn:
            near(3, ch).start()

    @pl.when(y == 2)
    def _():
        around().start()

    @pl.when(core == 1)
    def _():
        for ch in range(CHUNKS):
            across(0, ch).start()

    @pl.when(jnp.logical_and(z_lo == 1, y == 2))
    def _():
        for ch in upper:
            aside(ch).start()

    def take_far(ch):
        far(ch).wait_recv()
        for j in (1, 3):
            @pl.when(jnp.logical_and(y < j, near_goes(j, ch)))
            def _(j=j):
                near(j, ch).start()

        @pl.when(core == 0)
        def _():
            across(3, ch).start()

    def take(j, ch, when):
        @pl.when(jnp.logical_and(chip + j <= 7, when))
        def _():
            remote(
                blocks.at[0, rows_of(ch)], blocks.at[2 * j, rows_of(ch)],
                gather_send.at[0, ch], gather_recv.at[2 * j, ch], y_up,
            ).wait_recv()
            if j != 2:
                @pl.when(relays(j, ch))
                def _():
                    relay(j, ch).start()
            across(j - 1 + core, ch).start()

    def early(j, ch):
        if j == 2:
            return jnp.logical_and(z_lo == 1, y == 1)
        last = jnp.logical_or(y == 1, y == 2) if j == 1 else y == 0
        return jnp.where(z_lo == 0, relays(j, ch), last)

    def build(lag, carry):
        t0 = table[pl.ds(2 * lag, 1), :]
        t1 = table[pl.ds(2 * lag + 1, 1), :]
        rows = pl.ds(pl.multiple_of(lag * BS, BS), BS)
        for g in range(HALF // BS):
            re = turned[0, :, pl.ds(g * BS, BS)]
            im = turned[1, :, pl.ds(g * BS, BS)]
            left[rows, pl.ds(g * BS, BS)] = (t0 * re + t1 * im).astype(jnp.bfloat16)
            left[rows, pl.ds(HALF + g * BS, BS)] = (t0 * im - t1 * re).astype(jnp.bfloat16)
        return carry

    def turn(g, carry):
        rows = pl.ds(pl.multiple_of(g * BS, BS), BS)
        for r in range(2):
            turned[r, :, rows] = blocks[0, pl.ds(pl.multiple_of(r * HALF + g * BS, BS), BS), :].astype(jnp.float32).T
        return carry

    lax.fori_loop(0, HALF // BS, turn, 0)
    table_copy.wait()
    lax.fori_loop(0, LAGS // 2, build, 0)

    @pl.when(y == 3)
    def _():
        around().wait_recv()
        around_on().start()

    for s in range(CHUNKS):
        @pl.when(z_lo == 0)
        def _(s=s):
            take_far(s)
        take(1, s, early(1, s) if s < CHUNKS // 2 else jnp.logical_and(early(1, s), jnp.logical_not(waits)))
        take(3, own_turn[s], jnp.logical_and(z_lo == 1, early(3, own_turn[s])))
        if s > 0:
            take(3, s - 1, jnp.logical_and(z_lo == 0, jnp.logical_and(relays(3, s - 1), y != 1)))
        if s == CHUNKS // 2 - 1:
            @pl.when(held)
            def _():
                for ch in upper:
                    near(1, ch).start()
        lax.fori_loop(LAGS // 2 + s * LAGS // 8, LAGS // 2 + (s + 1) * LAGS // 8, build, 0)

    def sibling_done(j):
        for ch in range(CHUNKS):
            across(j, ch).wait_recv()

    @pl.when(z_lo == 1)
    def _():
        for ch in range(CHUNKS):
            take(2, ch, early(2, ch))
        for j in range(4):
            @pl.when(jnp.logical_and(core == 0, y == 3 - j))
            def _(j=j):
                sibling_done(j)

    def pass_on(ch, yy):
        take(3, ch, jnp.logical_and(z_lo == 0, y == yy))

    def take_late(j, ch):
        take(j, ch, jnp.logical_not(early(j, ch)))

    def gather_rest():
        @pl.when(jnp.logical_and(z_lo == 1, y == 3))
        def _():
            for ch in upper:
                aside(ch).wait_recv()
                aside_on(ch).start()

        for j in (3, 2):
            for ch in upper:
                take_late(j, ch)
        for j in range(4):
            taken = jnp.logical_and(z_lo == 1, jnp.logical_and(core == 0, y == 3 - j))

            @pl.when(jnp.logical_and(chip + j + core <= 7, jnp.logical_not(taken)))
            def _(j=j):
                sibling_done(j)

    def pieces_of(k):
        return 2 if k == K - 1 else 1

    def hop(k, way, kind):
        used = pl.ds(0, HX)
        if kind >= 2:
            size = HX // pieces_of(k) + TAIL
            used = pl.ds((kind - 2) * size, size)
        place = min(kind, 2)
        return remote(
            go.at[k, way, place, used], come.at[k, way, place, used],
            x_send.at[k, way, kind], x_recv.at[k, way, kind], x_down if way else x_up,
        )

    def z_copy(k, ee):
        return remote(
            zsums.at[k, ee - 1], zgot.at[k, ee - 1], z_send.at[k, ee - 1], z_recv.at[k, ee - 1],
            at_band(x, (z_hi + ee) % 4),
        )

    square = (BS, BS)
    diagonal = lax.broadcasted_iota(jnp.int32, square, 0) == lax.broadcasted_iota(jnp.int32, square, 1)
    tail_row = lax.broadcasted_iota(jnp.int32, (TAIL, BS), 0)

    def pack(message, lags, value_of):
        tail = jnp.zeros((TAIL, BS), jnp.float32)
        for lag in range(lags):
            value = value_of(lag)
            rounded = value.astype(jnp.bfloat16)
            message[pl.ds(lag * BS, BS), :] = rounded
            rest = jnp.where(diagonal, value - rounded.astype(jnp.float32), 0.0)
            tail = jnp.where(tail_row == lag, jnp.sum(rest, axis=0, keepdims=True), tail)
        message[pl.ds(lags * BS, TAIL), :] = tail.astype(jnp.bfloat16)

    def plain(message, value_of):
        for lag in range(4):
            message[pl.ds(lag * BS, BS), :] = value_of(lag).astype(jnp.bfloat16)

    def unpack(message, lags, lag):
        tail = message[pl.ds(lags * BS, TAIL), :].astype(jnp.float32)[lag:lag + 1]
        return message[pl.ds(lag * BS, BS), :].astype(jnp.float32) + jnp.where(diagonal, tail, 0.0)

    def rows_at(place):
        return pl.ds(pl.multiple_of(place * BS, BS), BS)

    def send_middle(k, way):
        plain(go.at[k, way, 0], lambda lag: part[k, 0, rows_at(way * 4 + lag), :])
        hop(k, way, 0).start()

    def sent(k, kind):
        for way in (0, 1):
            hop(k, way, kind).wait_send()

    def send_straight(k, way):
        plain(go.at[k, way, 1], lambda lag: part[k, 1 + way, rows_at((1 - way) * 4 + lag), :])
        hop(k, way, 1).start()

    def send_summed(k):
        count = 4 // pieces_of(k)
        size = HX // pieces_of(k) + TAIL
        for piece in range(pieces_of(k)):
            for way in (0, 1):
                def both(lag, way=way, at=piece * count):
                    through = come[k, way, 0, rows_at(at + lag), :].astype(jnp.float32)
                    return part[k, 1 + way, rows_at(way * 4 + at + lag), :] + through

                if piece == 0:
                    hop(k, way, 0).wait_recv()
                pack(go.at[k, way, 2, pl.ds(piece * size, size)], count, both)
                hop(k, way, 2 + piece).start()

    def reduce_x(k):
        count = 4 // pieces_of(k)
        size = HX // pieces_of(k) + TAIL
        for way in (0, 1):
            hop(k, way, 1).wait_recv()
        for piece in range(pieces_of(k)):
            for way in (0, 1):
                hop(k, way, 2 + piece).wait_recv()
                for lag in range(count):
                    at = piece * count + lag
                    rows = rows_at(way * 4 + at)
                    straight = come[k, 1 - way, 1, rows_at(at), :].astype(jnp.float32)
                    summed = unpack(come.at[k, way, 2, pl.ds(piece * size, size)], count, lag)
                    part[k, 3, rows, :] = part[k, 3, rows, :] + straight + summed
            if pieces_of(k) == 1:
                for ee in (2, 1, 3):
                    send_z(k, ee)
            else:
                for e in (piece, 2 + piece):
                    @pl.when(e != z_hi)
                    def _(e=e):
                        send_z(k, (e + 4 - z_hi) % 4)

    def send_z(k, ee):
        e = (z_hi + ee) % 4
        pack(zsums.at[k, ee - 1], 2, lambda lag: part[k, 3, rows_at(e * 2 + lag), :])
        z_copy(k, ee).start()

    def give(lag, k):
        return pltpu.make_async_copy(done.at[lag, k], out.at[lag, 0, k], done_sem.at[lag, k])

    def finish(k):
        for ee in (1, 3, 2):
            z_copy(k, ee).wait_recv()
        for lag in range(2):
            total = part[k, 3, rows_at(z_hi * 2 + lag), :]
            for s in range(3):
                total += unpack(zgot.at[k, s], 2, lag)
            done[lag, k] = (total * SCALE).astype(jnp.bfloat16)
            give(lag, k).start()

    def pick(t, values):
        chosen = jnp.int32(values[-1])
        for at in range(len(values) - 1):
            chosen = jnp.where(t == at, values[at], chosen)
        return chosen

    def multiply(slots, *after):
        width = len(slots) * BS

        def step(t, carry):
            q = pick(t, (0, 0, 1, 2, 1, 2, 3, 3))
            high = pick(t, (0, 1, 1, 0, 0, 1, 0, 1))
            ahead = pick(t, (2, 2, 1, 3, 1, 3, 0, 0))
            rows = pl.ds(pl.multiple_of(((x + ahead) % 4 * 2 + high) * HX, HX), HX)
            total = jnp.dot(left[rows, :], right[:, pl.ds(0, width)], preferred_element_type=jnp.float32)
            for n, k in enumerate(slots):
                part[k, q, pl.ds(pl.multiple_of(high * HX, HX), HX), :] = total[:, n * BS:(n + 1) * BS]
            for at, then in enumerate(after):
                pl.when(t == at)(then)
            return carry

        lax.fori_loop(0, 8, step, 0)

    def run(*steps):
        def then():
            for step in steps:
                step[0](*step[1:])

        return then

    right[:, pl.ds(0, BS)] = blocks[jnp.minimum(REACH, 15 - fibre)]
    multiply(
        (0,),
        run((send_middle, 0, 0), (pass_on, 3, 0)),
        run((send_middle, 0, 1), (pass_on, 2, 1), (pass_on, 3, 2), (take, 1, 2, waits)),
        run((send_straight, 0, 0)),
        run((send_straight, 0, 1), (pass_on, 3, 1), (take, 1, 3, waits)),
        run(),
        run((take_late, 3, 0), (take_late, 3, 1)),
        run(*((take_late, 1, ch) for ch in range(CHUNKS))),
        run((send_summed, 0), (take_late, 2, 0), (take_late, 2, 1)),
    )
    gather_rest()
    for n, slot in enumerate((1, 2)):
        right[:, pl.ds(n * BS, BS)] = blocks[offsets[0, slot]]
    multiply(
        (1, 2),
        run((send_middle, 1, 0)),
        run((send_middle, 1, 1)),
        run((send_straight, 1, 0)),
        run((send_straight, 1, 1)),
        run((send_middle, 2, 0), (send_middle, 2, 1)),
        run(),
        run((send_summed, 1)),
        run((send_straight, 2, 0), (send_straight, 2, 1), (reduce_x, 0)),
    )
    right[:, pl.ds(0, BS)] = blocks[offsets[0, 3]]
    multiply(
        (3,),
        run(),
        run((send_summed, 2), (reduce_x, 1), (sent, 2, 1), (send_middle, 3, 0), (send_middle, 3, 1)),
        run(),
        run((sent, 2, 2), (send_straight, 3, 0), (send_straight, 3, 1)),
        run((reduce_x, 2)),
        run(),
        run((finish, 0)),
        run((send_summed, 3)),
    )
    finish(1)
    reduce_x(3)
    finish(2)
    finish(3)

    @pl.when(y >= 2)
    def _():
        around().wait_send()

    @pl.when(jnp.logical_and(z_lo == 1, y >= 2))
    def _():
        for ch in upper:
            aside(ch).wait_send()

    @pl.when(z_lo == 1)
    def _():
        for ch in range(CHUNKS):
            far(ch).wait_send()

    for j in (1, 3):
        for ch in range(CHUNKS):
            @pl.when(near_goes(j, ch))
            def _(j=j, ch=ch):
                near(j, ch).wait_send()

            @pl.when(relays(j, ch))
            def _(j=j, ch=ch):
                relay(j, ch).wait_send()

    for j in range(4):
        @pl.when(chip + j + (1 - core) <= 7)
        def _(j=j):
            for ch in range(CHUNKS):
                across(j, ch).wait_send()

    for k in range(K):
        for way in (0, 1):
            for kind in range(2 + pieces_of(k)):
                if k != 2 or kind == 0:
                    hop(k, way, kind).wait_send()
        for ee in (1, 2, 3):
            z_copy(k, ee).wait_send()
        for lag in range(2):
            give(lag, k).wait()


def on_device(spectra, dead_mask, partner_offset):
    vmem = pl.BlockSpec(memory_space=pltpu.VMEM)
    bf16, f32 = jnp.bfloat16, jnp.float32
    return pl.pallas_call(
        kernel,
        out_shape=jax.ShapeDtypeStruct((LAGS // BANDS, 1, K, BS, BS), bf16),
        in_specs=[pl.BlockSpec(memory_space=pl.ANY), vmem, pl.BlockSpec(memory_space=pltpu.SMEM), pl.BlockSpec(memory_space=pl.ANY)],
        out_specs=pl.BlockSpec(memory_space=pl.ANY),
        scratch_shapes=[
            pltpu.VMEM((DEPTH, BS), bf16),
            pltpu.VMEM((LAGS // BANDS, K, BS, BS), bf16),
            pltpu.SemaphoreType.DMA,
            pltpu.SemaphoreType.DMA((LAGS // BANDS, K)),
            pltpu.VMEM((REACH + 1, DEPTH, BS), bf16),
            pltpu.VMEM((CROWS, BS), bf16),
            pltpu.VMEM((2, BS, HALF), f32),
            pltpu.VMEM((LAGS * BS, DEPTH), bf16),
            pltpu.VMEM((DEPTH, 2 * BS), bf16),
            pltpu.VMEM((2 * LAGS, BS), f32),
            pltpu.VMEM((K, 4, XROWS, BS), f32),
            pltpu.VMEM((K, 2, 3, HX + 2 * TAIL, BS), bf16),
            pltpu.VMEM((K, 2, 3, HX + 2 * TAIL, BS), bf16),
            pltpu.VMEM((K, 3, ZROWS + TAIL, BS), bf16),
            pltpu.VMEM((K, 3, ZROWS + TAIL, BS), bf16),
            pltpu.SemaphoreType.DMA,
            pltpu.SemaphoreType.DMA((4, CHUNKS)),
            pltpu.SemaphoreType.DMA((2, CHUNKS)),
            pltpu.SemaphoreType.DMA((CHUNKS,)),
            pltpu.SemaphoreType.DMA,
            pltpu.SemaphoreType.DMA,
            pltpu.SemaphoreType.DMA((REACH + 1, CHUNKS)),
            pltpu.SemaphoreType.DMA((4, CHUNKS)),
            pltpu.SemaphoreType.DMA((K, 2, 4)),
            pltpu.SemaphoreType.DMA((K, 2, 4)),
            pltpu.SemaphoreType.DMA((K, 3)),
            pltpu.SemaphoreType.DMA((K, 3)),
        ],
        compiler_params=pltpu.CompilerParams(
            collective_id=0, has_side_effects=True, vmem_limit_bytes=56 * 1024 * 1024
        ),
        cost_estimate=pl.CostEstimate(
            flops=2 * LAGS * BS * DEPTH * K * BS, bytes_accessed=1 << 20, transcendentals=0
        ),
    )(spectra.reshape(DEPTH, BS), dead_mask.reshape(1, BS), partner_offset, jnp.asarray(lag_table()))


def solution(mesh):
    in_specs = (P(None, None, "band", "fibre"), P("fibre"), P("fibre", None))
    out_specs = P("band", "fibre", None, None, None)
    return jax.shard_map(
        on_device, mesh=mesh, in_specs=in_specs, out_specs=out_specs, check_vma=False
    )
```

```python
import functools
import math

import jax
import jax.numpy as jnp
import ml_dtypes
import numpy as np
from jax import lax
from jax.experimental import pallas as pl
from jax.experimental.pallas import tpu as pltpu
from jax.sharding import PartitionSpec as P

BS = 128
NF = 512
REACH = 8
K = 4
W = 32
LAGS = 32
BANDS = 16
BINS = NF // BANDS
DEPTH = 2 * W * BINS
HALF = W * BINS
CHUNKS = 4
CROWS = DEPTH // CHUNKS
XROWS = LAGS // 4 * BS
HX = XROWS // 2
ZROWS = LAGS // 16 * BS
TAIL = 16
SCALE = 1.0 / math.sqrt(W) / math.sqrt(NF)


def lag_table():
    bins = np.arange(NF)[:, None]
    lags = np.arange(LAGS)[None, :] - LAGS // 2
    angles = (bins * lags % (2 * NF)) * (math.pi / NF)
    table = np.stack([np.cos(angles), -np.sin(angles)], axis=2)
    table = table.astype(np.float32).astype(ml_dtypes.bfloat16).astype(np.float32)
    table = table.reshape(BANDS, BINS, 2 * LAGS).transpose(0, 2, 1)
    return np.tile(table, (1, 1, BS // BINS))


def kernel(
    spectra, mask, offsets, tables, out,
    raw, done, raw_sem, done_sem, blocks, spare, turned, left, right, table, part, go, come, zsums, zgot,
    table_sem, gather_send, relay_send, aside_send, around_send, around_recv, gather_recv, sib_send, x_send, x_recv, z_send, z_recv,
):
    fibre, band = lax.axis_index("fibre"), lax.axis_index("band")
    z_lo, y, core = fibre // 8, fibre // 2 % 4, fibre % 2
    chip = fibre // 2
    x, z_hi = band // 4, band % 4

    def at_fibre(zz, yy, cc):
        return {"fibre": (zz * 4 + yy) * 2 + cc, "band": band}

    def at_band(xx, zz):
        return {"fibre": fibre, "band": xx * 4 + zz}

    sibling = at_fibre(z_lo, y, 1 - core)
    other_z = at_fibre(1 - z_lo, y, core)
    y_down, y_up = at_fibre(z_lo, (y + 3) % 4, core), at_fibre(z_lo, (y + 1) % 4, core)
    x_down, x_up = at_band((x + 3) % 4, z_hi), at_band((x + 1) % 4, z_hi)
    raw_copy = pltpu.make_async_copy(spectra, raw, raw_sem)
    raw_copy.start()
    barrier = pltpu.get_barrier_semaphore()
    peers = [sibling, other_z, y_down, y_up, x_down, x_up]
    peers += [at_band(x, (z_hi + j) % 4) for j in (1, 2, 3)]
    for peer in peers:
        pl.semaphore_signal(barrier, inc=1, device_id=peer, device_id_type=pl.DeviceIdType.MESH)

    table_copy = pltpu.make_async_copy(tables.at[band], table, table_sem)
    table_copy.start()
    alive = mask[...].astype(jnp.bfloat16)
    raw_copy.wait()
    blocks[0] = raw[...] * alive
    pl.semaphore_wait(barrier, len(peers))

    def remote(src, dst, send, recv, device):
        return pltpu.make_async_remote_copy(
            src_ref=src, dst_ref=dst, send_sem=send, recv_sem=recv,
            device_id=device, device_id_type=pl.DeviceIdType.MESH,
        )

    def rows_of(ch):
        return pl.ds(ch * CROWS, CROWS)

    def far(ch):
        return remote(
            blocks.at[0, rows_of(ch)], blocks.at[8, rows_of(ch)],
            gather_send.at[0, ch], gather_recv.at[8, ch], other_z,
        )

    def near(j, ch):
        src = jnp.where(y >= j, 0, 8)
        return remote(
            blocks.at[src, rows_of(ch)], blocks.at[2 * j, rows_of(ch)],
            gather_send.at[j, ch], gather_recv.at[2 * j, ch], y_down if j == 1 else y_up,
        )

    def relay(j, ch):
        return remote(
            blocks.at[2 * j, rows_of(ch)], blocks.at[4, rows_of(ch)],
            relay_send.at[j // 2, ch], gather_recv.at[4, ch], y_down if j == 1 else y_up,
        )

    def across(j, ch):
        return remote(
            blocks.at[2 * j + 2 * (1 - core), rows_of(ch)], blocks.at[2 * j + 1, rows_of(ch)],
            sib_send.at[j, ch], gather_recv.at[2 * j + 1, ch], sibling,
        )

    def aside(ch):
        return remote(
            blocks.at[0, rows_of(ch)], blocks.at[8, rows_of(ch)],
            aside_send.at[ch], gather_recv.at[8, ch], y_up,
        )

    def aside_on(ch):
        return remote(
            blocks.at[8, rows_of(ch)], blocks.at[6, rows_of(ch)],
            aside_send.at[ch], gather_recv.at[6, ch], other_z,
        )

    upper = range(CHUNKS // 2, CHUNKS)
    last_rows = rows_of(CHUNKS - 1)

    def around():
        return remote(blocks.at[0, last_rows], spare, around_send, around_recv, y_up)

    def around_on():
        return remote(spare, blocks.at[4, last_rows], around_send, gather_recv.at[4, CHUNKS - 1], y_up)

    def relays(j, ch):
        last = ch == CHUNKS - 1
        low = z_lo == 0
        if j == 1:
            goes = [jnp.logical_and(y >= 1, not last)]
            if ch == 2:
                goes = [jnp.logical_or(y == 1, jnp.logical_and(low, y >= 2))]
        else:
            goes = [y == 2, jnp.logical_and(y == 0, jnp.logical_or(last, jnp.logical_and(ch == 2, jnp.logical_not(low))))]
            goes.append(jnp.logical_and(y == 1, last))
        goes = functools.reduce(jnp.logical_or, goes)
        return jnp.logical_and(chip + j <= 7, goes)

    def near_goes(j, ch):
        limit = 1 if j == 1 else 2 if ch in upper else 3
        return jnp.logical_or(y >= j, jnp.logical_and(z_lo == 0, y < limit))

    @pl.when(z_lo == 1)
    def _():
        for ch in range(CHUNKS):
            far(ch).start()

    own_turn = [*upper, *range(CHUNKS // 2)]
    held = jnp.logical_and(z_lo == 1, y == 2)
    waits = jnp.logical_and(z_lo == 1, y == 1)

    @pl.when(y >= 1)
    def _():
        for ch in range(CHUNKS // 2):
            near(1, ch).start()

    @pl.when(jnp.logical_and(y >= 1, jnp.logical_not(held)))
    def _():
        for ch in upper:
            near(1, ch).start()

    @pl.when(y == 3)
    def _():
        for ch in own_turn:
            near(3, ch).start()

    @pl.when(y == 2)
    def _():
        around().start()

    @pl.when(core == 1)
    def _():
        for ch in range(CHUNKS):
            across(0, ch).start()

    @pl.when(jnp.logical_and(z_lo == 1, y == 2))
    def _():
        for ch in upper:
            aside(ch).start()

    def take_far(ch):
        far(ch).wait_recv()
        for j in (1, 3):
            @pl.when(jnp.logical_and(y < j, near_goes(j, ch)))
            def _(j=j):
                near(j, ch).start()

        @pl.when(core == 0)
        def _():
            across(3, ch).start()

    def take(j, ch, when):
        @pl.when(jnp.logical_and(chip + j <= 7, when))
        def _():
            remote(
                blocks.at[0, rows_of(ch)], blocks.at[2 * j, rows_of(ch)],
                gather_send.at[0, ch], gather_recv.at[2 * j, ch], y_up,
            ).wait_recv()
            if j != 2:
                @pl.when(relays(j, ch))
                def _():
                    relay(j, ch).start()
            across(j - 1 + core, ch).start()

    def early(j, ch):
        if j == 2:
            return jnp.logical_and(z_lo == 1, y == 1)
        last = jnp.logical_or(y == 1, y == 2) if j == 1 else y == 0
        return jnp.where(z_lo == 0, relays(j, ch), last)

    def build(lag, carry):
        t0 = table[pl.ds(2 * lag, 1), :]
        t1 = table[pl.ds(2 * lag + 1, 1), :]
        rows = pl.ds(pl.multiple_of(lag * BS, BS), BS)
        for g in range(HALF // BS):
            re = turned[0, :, pl.ds(g * BS, BS)]
            im = turned[1, :, pl.ds(g * BS, BS)]
            left[rows, pl.ds(g * BS, BS)] = (t0 * re + t1 * im).astype(jnp.bfloat16)
            left[rows, pl.ds(HALF + g * BS, BS)] = (t0 * im - t1 * re).astype(jnp.bfloat16)
        return carry

    def turn(g, carry):
        rows = pl.ds(pl.multiple_of(g * BS, BS), BS)
        for r in range(2):
            turned[r, :, rows] = blocks[0, pl.ds(pl.multiple_of(r * HALF + g * BS, BS), BS), :].astype(jnp.float32).T
        return carry

    lax.fori_loop(0, HALF // BS, turn, 0)
    table_copy.wait()
    lax.fori_loop(0, LAGS // 2, build, 0)

    for s in range(CHUNKS):
        @pl.when(z_lo == 0)
        def _(s=s):
            take_far(s)
        take(1, s, early(1, s) if s < CHUNKS // 2 else jnp.logical_and(early(1, s), jnp.logical_not(jnp.logical_or(waits, y >= 3 - (z_lo == 0).astype(jnp.int32)))))
        take(3, own_turn[s], jnp.logical_and(z_lo == 1, early(3, own_turn[s])))
        if s > 0:
            take(3, s - 1, jnp.logical_and(z_lo == 0, jnp.logical_and(relays(3, s - 1), y != 1)))
        if s == CHUNKS // 2 - 1:
            @pl.when(held)
            def _():
                for ch in upper:
                    near(1, ch).start()
        lax.fori_loop(LAGS // 2 + s * LAGS // 8, LAGS // 2 + (s + 1) * LAGS // 8, build, 0)

    @pl.when(y == 3)
    def _():
        around().wait_recv()
        around_on().start()

    def sibling_done(j):
        for ch in range(CHUNKS):
            across(j, ch).wait_recv()

    @pl.when(z_lo == 1)
    def _():
        for ch in range(CHUNKS):
            take(2, ch, early(2, ch))
        for j in range(4):
            @pl.when(jnp.logical_and(core == 0, y == 3 - j))
            def _(j=j):
                sibling_done(j)

    def pass_on(ch, yy):
        take(3, ch, jnp.logical_and(z_lo == 0, y == yy))

    def take_late(j, ch):
        take(j, ch, jnp.logical_not(early(j, ch)))

    def gather_rest():
        @pl.when(jnp.logical_and(z_lo == 1, y == 3))
        def _():
            for ch in upper:
                aside(ch).wait_recv()
                aside_on(ch).start()

        for j in (1, 3, 2):
            for ch in range(CHUNKS):
                take_late(j, ch)
        for j in range(4):
            taken = jnp.logical_and(z_lo == 1, jnp.logical_and(core == 0, y == 3 - j))

            @pl.when(jnp.logical_and(chip + j + core <= 7, jnp.logical_not(taken)))
            def _(j=j):
                sibling_done(j)

    def pieces_of(k):
        return 2 if k == K - 1 else 1

    def hop(k, way, kind):
        used = pl.ds(0, HX)
        if kind >= 2:
            size = HX // pieces_of(k) + TAIL
            used = pl.ds((kind - 2) * size, size)
        place = min(kind, 2)
        return remote(
            go.at[k, way, place, used], come.at[k, way, place, used],
            x_send.at[k, way, kind], x_recv.at[k, way, kind], x_down if way else x_up,
        )

    def z_copy(k, ee):
        return remote(
            zsums.at[k, ee - 1], zgot.at[k, ee - 1], z_send.at[k, ee - 1], z_recv.at[k, ee - 1],
            at_band(x, (z_hi + ee) % 4),
        )

    square = (BS, BS)
    diagonal = lax.broadcasted_iota(jnp.int32, square, 0) == lax.broadcasted_iota(jnp.int32, square, 1)
    tail_row = lax.broadcasted_iota(jnp.int32, (TAIL, BS), 0)

    def pack(message, lags, value_of):
        tail = jnp.zeros((TAIL, BS), jnp.float32)
        for lag in range(lags):
            value = value_of(lag)
            rounded = value.astype(jnp.bfloat16)
            message[pl.ds(lag * BS, BS), :] = rounded
            rest = jnp.where(diagonal, value - rounded.astype(jnp.float32), 0.0)
            tail = jnp.where(tail_row == lag, jnp.sum(rest, axis=0, keepdims=True), tail)
        message[pl.ds(lags * BS, TAIL), :] = tail.astype(jnp.bfloat16)

    def plain(message, value_of):
        for lag in range(4):
            message[pl.ds(lag * BS, BS), :] = value_of(lag).astype(jnp.bfloat16)

    def unpack(message, lags, lag):
        tail = message[pl.ds(lags * BS, TAIL), :].astype(jnp.float32)[lag:lag + 1]
        return message[pl.ds(lag * BS, BS), :].astype(jnp.float32) + jnp.where(diagonal, tail, 0.0)

    def rows_at(place):
        return pl.ds(pl.multiple_of(place * BS, BS), BS)

    def send_middle(k, way):
        plain(go.at[k, way, 0], lambda lag: part[k, 0, rows_at(way * 4 + lag), :])
        hop(k, way, 0).start()

    def sent(k, kind):
        for way in (0, 1):
            hop(k, way, kind).wait_send()

    def send_straight(k, way):
        plain(go.at[k, way, 1], lambda lag: part[k, 1 + way, rows_at((1 - way) * 4 + lag), :])
        hop(k, way, 1).start()

    def send_summed(k):
        count = 4 // pieces_of(k)
        size = HX // pieces_of(k) + TAIL
        for piece in range(pieces_of(k)):
            for way in (0, 1):
                def both(lag, way=way, at=piece * count):
                    through = come[k, way, 0, rows_at(at + lag), :].astype(jnp.float32)
                    return part[k, 1 + way, rows_at(way * 4 + at + lag), :] + through

                if piece == 0:
                    hop(k, way, 0).wait_recv()
                pack(go.at[k, way, 2, pl.ds(piece * size, size)], count, both)
                hop(k, way, 2 + piece).start()

    def reduce_x(k):
        count = 4 // pieces_of(k)
        size = HX // pieces_of(k) + TAIL
        for way in (0, 1):
            hop(k, way, 1).wait_recv()
        for piece in range(pieces_of(k)):
            for way in (0, 1):
                hop(k, way, 2 + piece).wait_recv()
                for lag in range(count):
                    at = piece * count + lag
                    rows = rows_at(way * 4 + at)
                    straight = come[k, 1 - way, 1, rows_at(at), :].astype(jnp.float32)
                    summed = unpack(come.at[k, way, 2, pl.ds(piece * size, size)], count, lag)
                    part[k, 3, rows, :] = part[k, 3, rows, :] + straight + summed
            if pieces_of(k) == 1:
                for ee in (2, 1, 3):
                    send_z(k, ee)
            else:
                for e in (piece, 2 + piece):
                    @pl.when(e != z_hi)
                    def _(e=e):
                        send_z(k, (e + 4 - z_hi) % 4)

    def send_z(k, ee):
        e = (z_hi + ee) % 4
        pack(zsums.at[k, ee - 1], 2, lambda lag: part[k, 3, rows_at(e * 2 + lag), :])
        z_copy(k, ee).start()

    def give(lag, k):
        return pltpu.make_async_copy(done.at[lag, k], out.at[lag, 0, k], done_sem.at[lag, k])

    def finish(k):
        for ee in (1, 3, 2):
            z_copy(k, ee).wait_recv()
        for lag in range(2):
            total = part[k, 3, rows_at(z_hi * 2 + lag), :]
            for s in range(3):
                total += unpack(zgot.at[k, s], 2, lag)
            done[lag, k] = (total * SCALE).astype(jnp.bfloat16)
            give(lag, k).start()

    def pick(t, values):
        chosen = jnp.int32(values[-1])
        for at in range(len(values) - 1):
            chosen = jnp.where(t == at, values[at], chosen)
        return chosen

    def multiply(slots, *after):
        width = len(slots) * BS

        def step(t, carry):
            q = pick(t, (0, 0, 1, 2, 1, 2, 3, 3))
            high = pick(t, (0, 1, 1, 0, 0, 1, 0, 1))
            ahead = pick(t, (2, 2, 1, 3, 1, 3, 0, 0))
            rows = pl.ds(pl.multiple_of(((x + ahead) % 4 * 2 + high) * HX, HX), HX)
            total = jnp.dot(left[rows, :], right[:, pl.ds(0, width)], preferred_element_type=jnp.float32)
            for n, k in enumerate(slots):
                part[k, q, pl.ds(pl.multiple_of(high * HX, HX), HX), :] = total[:, n * BS:(n + 1) * BS]
            for at, then in enumerate(after):
                pl.when(t == at)(then)
            return carry

        lax.fori_loop(0, 8, step, 0)

    def run(*steps):
        def then():
            for step in steps:
                step[0](*step[1:])

        return then

    right[:, pl.ds(0, BS)] = blocks[jnp.minimum(REACH, 15 - fibre)]
    multiply(
        (0,),
        run((send_middle, 0, 0), (pass_on, 3, 0), (take, 1, 2, jnp.logical_and(z_lo == 0, y >= 2))),
        run((send_middle, 0, 1), (pass_on, 3, 2), (take, 1, 2, waits)),
        run((send_straight, 0, 0)),
        run((send_straight, 0, 1), (pass_on, 3, 1), (take, 1, 3, waits)),
        run(),
        run(),
        run(),
        run((send_summed, 0)),
    )
    gather_rest()
    for n, slot in enumerate((1, 2)):
        right[:, pl.ds(n * BS, BS)] = blocks[offsets[0, slot]]
    multiply(
        (1, 2),
        run((send_middle, 1, 0)),
        run((send_middle, 1, 1)),
        run((send_straight, 1, 0)),
        run((send_straight, 1, 1)),
        run((send_middle, 2, 0), (send_middle, 2, 1)),
        run(),
        run((send_summed, 1)),
        run((send_straight, 2, 0), (send_straight, 2, 1), (reduce_x, 0)),
    )
    right[:, pl.ds(0, BS)] = blocks[offsets[0, 3]]
    multiply(
        (3,),
        run(),
        run((send_summed, 2), (reduce_x, 1), (sent, 2, 1), (send_middle, 3, 0), (send_middle, 3, 1)),
        run(),
        run((sent, 2, 2), (send_straight, 3, 0), (send_straight, 3, 1)),
        run((reduce_x, 2)),
        run(),
        run((finish, 0)),
        run((send_summed, 3)),
    )
    finish(1)
    reduce_x(3)
    finish(2)
    finish(3)

    @pl.when(y >= 2)
    def _():
        around().wait_send()

    @pl.when(jnp.logical_and(z_lo == 1, y >= 2))
    def _():
        for ch in upper:
            aside(ch).wait_send()

    @pl.when(z_lo == 1)
    def _():
        for ch in range(CHUNKS):
            far(ch).wait_send()

    for j in (1, 3):
        for ch in range(CHUNKS):
            @pl.when(near_goes(j, ch))
            def _(j=j, ch=ch):
                near(j, ch).wait_send()

            @pl.when(relays(j, ch))
            def _(j=j, ch=ch):
                relay(j, ch).wait_send()

    for j in range(4):
        @pl.when(chip + j + (1 - core) <= 7)
        def _(j=j):
            for ch in range(CHUNKS):
                across(j, ch).wait_send()

    for k in range(K):
        for way in (0, 1):
            for kind in range(2 + pieces_of(k)):
                if k != 2 or kind == 0:
                    hop(k, way, kind).wait_send()
        for ee in (1, 2, 3):
            z_copy(k, ee).wait_send()
        for lag in range(2):
            give(lag, k).wait()


def on_device(spectra, dead_mask, partner_offset):
    vmem = pl.BlockSpec(memory_space=pltpu.VMEM)
    bf16, f32 = jnp.bfloat16, jnp.float32
    return pl.pallas_call(
        kernel,
        out_shape=jax.ShapeDtypeStruct((LAGS // BANDS, 1, K, BS, BS), bf16),
        in_specs=[pl.BlockSpec(memory_space=pl.ANY), vmem, pl.BlockSpec(memory_space=pltpu.SMEM), pl.BlockSpec(memory_space=pl.ANY)],
        out_specs=pl.BlockSpec(memory_space=pl.ANY),
        scratch_shapes=[
            pltpu.VMEM((DEPTH, BS), bf16),
            pltpu.VMEM((LAGS // BANDS, K, BS, BS), bf16),
            pltpu.SemaphoreType.DMA,
            pltpu.SemaphoreType.DMA((LAGS // BANDS, K)),
            pltpu.VMEM((REACH + 1, DEPTH, BS), bf16),
            pltpu.VMEM((CROWS, BS), bf16),
            pltpu.VMEM((2, BS, HALF), f32),
            pltpu.VMEM((LAGS * BS, DEPTH), bf16),
            pltpu.VMEM((DEPTH, 2 * BS), bf16),
            pltpu.VMEM((2 * LAGS, BS), f32),
            pltpu.VMEM((K, 4, XROWS, BS), f32),
            pltpu.VMEM((K, 2, 3, HX + 2 * TAIL, BS), bf16),
            pltpu.VMEM((K, 2, 3, HX + 2 * TAIL, BS), bf16),
            pltpu.VMEM((K, 3, ZROWS + TAIL, BS), bf16),
            pltpu.VMEM((K, 3, ZROWS + TAIL, BS), bf16),
            pltpu.SemaphoreType.DMA,
            pltpu.SemaphoreType.DMA((4, CHUNKS)),
            pltpu.SemaphoreType.DMA((2, CHUNKS)),
            pltpu.SemaphoreType.DMA((CHUNKS,)),
            pltpu.SemaphoreType.DMA,
            pltpu.SemaphoreType.DMA,
            pltpu.SemaphoreType.DMA((REACH + 1, CHUNKS)),
            pltpu.SemaphoreType.DMA((4, CHUNKS)),
            pltpu.SemaphoreType.DMA((K, 2, 4)),
            pltpu.SemaphoreType.DMA((K, 2, 4)),
            pltpu.SemaphoreType.DMA((K, 3)),
            pltpu.SemaphoreType.DMA((K, 3)),
        ],
        compiler_params=pltpu.CompilerParams(
            collective_id=0, has_side_effects=True, vmem_limit_bytes=56 * 1024 * 1024
        ),
        cost_estimate=pl.CostEstimate(
            flops=2 * LAGS * BS * DEPTH * K * BS, bytes_accessed=1 << 20, transcendentals=0
        ),
    )(spectra.reshape(DEPTH, BS), dead_mask.reshape(1, BS), partner_offset, jnp.asarray(lag_table()))


def solution(mesh):
    in_specs = (P(None, None, "band", "fibre"), P("fibre"), P("fibre", None))
    out_specs = P("band", "fibre", None, None, None)
    return jax.shard_map(
        on_device, mesh=mesh, in_specs=in_specs, out_specs=out_specs, check_vma=False
    )
```

```python
import functools
import math

import jax
import jax.numpy as jnp
import ml_dtypes
import numpy as np
from jax import lax
from jax.experimental import pallas as pl
from jax.experimental.pallas import tpu as pltpu
from jax.sharding import PartitionSpec as P

BS = 128
NF = 512
REACH = 8
K = 4
W = 32
LAGS = 32
BANDS = 16
BINS = NF // BANDS
DEPTH = 2 * W * BINS
HALF = W * BINS
CHUNKS = 4
CROWS = DEPTH // CHUNKS
XROWS = LAGS // 4 * BS
HX = XROWS // 2
ZROWS = LAGS // 16 * BS
TAIL = 16
SCALE = 1.0 / math.sqrt(W) / math.sqrt(NF)


def lag_table():
    bins = np.arange(NF)[:, None]
    lags = np.arange(LAGS)[None, :] - LAGS // 2
    angles = (bins * lags % (2 * NF)) * (math.pi / NF)
    table = np.stack([np.cos(angles), -np.sin(angles)], axis=2)
    table = table.astype(np.float32).astype(ml_dtypes.bfloat16).astype(np.float32)
    table = table.reshape(BANDS, BINS, 2 * LAGS).transpose(0, 2, 1)
    return np.tile(table, (1, 1, BS // BINS))


def kernel(
    spectra, mask, offsets, tables, out,
    raw, done, raw_sem, done_sem, blocks, spare, turned, left, right, table, part, go, come, zsums, zgot,
    table_sem, gather_send, relay_send, aside_send, around_send, around_recv, gather_recv, sib_send, x_send, x_recv, z_send, z_recv,
):
    fibre, band = lax.axis_index("fibre"), lax.axis_index("band")
    z_lo, y, core = fibre // 8, fibre // 2 % 4, fibre % 2
    chip = fibre // 2
    x, z_hi = band // 4, band % 4

    def at_fibre(zz, yy, cc):
        return {"fibre": (zz * 4 + yy) * 2 + cc, "band": band}

    def at_band(xx, zz):
        return {"fibre": fibre, "band": xx * 4 + zz}

    sibling = at_fibre(z_lo, y, 1 - core)
    other_z = at_fibre(1 - z_lo, y, core)
    y_down, y_up = at_fibre(z_lo, (y + 3) % 4, core), at_fibre(z_lo, (y + 1) % 4, core)
    x_down, x_up = at_band((x + 3) % 4, z_hi), at_band((x + 1) % 4, z_hi)
    raw_copy = pltpu.make_async_copy(spectra, raw, raw_sem)
    raw_copy.start()
    barrier = pltpu.get_barrier_semaphore()
    peers = [sibling, other_z, y_down, y_up, x_down, x_up]
    peers += [at_band(x, (z_hi + j) % 4) for j in (1, 2, 3)]
    for peer in peers:
        pl.semaphore_signal(barrier, inc=1, device_id=peer, device_id_type=pl.DeviceIdType.MESH)

    table_copy = pltpu.make_async_copy(tables.at[band], table, table_sem)
    table_copy.start()
    alive = mask[...].astype(jnp.bfloat16)
    raw_copy.wait()
    blocks[0] = raw[...] * alive
    pl.semaphore_wait(barrier, len(peers))

    def remote(src, dst, send, recv, device):
        return pltpu.make_async_remote_copy(
            src_ref=src, dst_ref=dst, send_sem=send, recv_sem=recv,
            device_id=device, device_id_type=pl.DeviceIdType.MESH,
        )

    def rows_of(ch):
        return pl.ds(ch * CROWS, CROWS)

    def far(ch):
        return remote(
            blocks.at[0, rows_of(ch)], blocks.at[8, rows_of(ch)],
            gather_send.at[0, ch], gather_recv.at[8, ch], other_z,
        )

    def near(j, ch):
        src = jnp.where(y >= j, 0, 8)
        return remote(
            blocks.at[src, rows_of(ch)], blocks.at[2 * j, rows_of(ch)],
            gather_send.at[j, ch], gather_recv.at[2 * j, ch], y_down if j == 1 else y_up,
        )

    def relay(j, ch):
        return remote(
            blocks.at[2 * j, rows_of(ch)], blocks.at[4, rows_of(ch)],
            relay_send.at[j // 2, ch], gather_recv.at[4, ch], y_down if j == 1 else y_up,
        )

    def across(j, ch):
        return remote(
            blocks.at[2 * j + 2 * (1 - core), rows_of(ch)], blocks.at[2 * j + 1, rows_of(ch)],
            sib_send.at[j, ch], gather_recv.at[2 * j + 1, ch], sibling,
        )

    def aside(ch):
        return remote(
            blocks.at[0, rows_of(ch)], blocks.at[8, rows_of(ch)],
            aside_send.at[ch], gather_recv.at[8, ch], y_up,
        )

    def aside_on(ch):
        return remote(
            blocks.at[8, rows_of(ch)], blocks.at[6, rows_of(ch)],
            aside_send.at[ch], gather_recv.at[6, ch], other_z,
        )

    upper = range(CHUNKS // 2, CHUNKS)
    last_rows = rows_of(CHUNKS - 1)

    def around():
        return remote(blocks.at[0, last_rows], spare, around_send, around_recv, y_up)

    def around_on():
        return remote(spare, blocks.at[4, last_rows], around_send, gather_recv.at[4, CHUNKS - 1], y_up)

    def relays(j, ch):
        last = ch == CHUNKS - 1
        low = z_lo == 0
        if j == 1:
            goes = [jnp.logical_and(y >= 1, not last)]
            if ch == 2:
                goes = [jnp.logical_or(y == 1, jnp.logical_and(low, y >= 2))]
        else:
            goes = [y == 2, jnp.logical_and(y == 0, jnp.logical_or(last, jnp.logical_and(ch == 2, jnp.logical_not(low))))]
            goes.append(jnp.logical_and(y == 1, last))
        goes = functools.reduce(jnp.logical_or, goes)
        return jnp.logical_and(chip + j <= 7, goes)

    def near_goes(j, ch):
        limit = 1 if j == 1 else 2 if ch in upper else 3
        return jnp.logical_or(y >= j, jnp.logical_and(z_lo == 0, y < limit))

    @pl.when(z_lo == 1)
    def _():
        for ch in range(CHUNKS):
            far(ch).start()

    own_turn = [*upper, *range(CHUNKS // 2)]
    held = jnp.logical_and(z_lo == 1, y == 2)
    waits = jnp.logical_and(z_lo == 1, y == 1)

    @pl.when(y >= 1)
    def _():
        for ch in range(CHUNKS // 2):
            near(1, ch).start()

    @pl.when(jnp.logical_and(y >= 1, jnp.logical_not(held)))
    def _():
        for ch in upper:
            near(1, ch).start()

    @pl.when(y == 3)
    def _():
        for ch in own_turn:
            near(3, ch).start()

    @pl.when(y == 2)
    def _():
        around().start()

    @pl.when(core == 1)
    def _():
        for ch in range(CHUNKS):
            across(0, ch).start()

    @pl.when(jnp.logical_and(z_lo == 1, y == 2))
    def _():
        for ch in upper:
            aside(ch).start()

    def take_far(ch):
        far(ch).wait_recv()
        for j in (1, 3):
            @pl.when(jnp.logical_and(y < j, near_goes(j, ch)))
            def _(j=j):
                near(j, ch).start()

        @pl.when(core == 0)
        def _():
            across(3, ch).start()

    def take(j, ch, when):
        @pl.when(jnp.logical_and(chip + j <= 7, when))
        def _():
            remote(
                blocks.at[0, rows_of(ch)], blocks.at[2 * j, rows_of(ch)],
                gather_send.at[0, ch], gather_recv.at[2 * j, ch], y_up,
            ).wait_recv()
            if j != 2:
                @pl.when(relays(j, ch))
                def _():
                    relay(j, ch).start()
            across(j - 1 + core, ch).start()

    def early(j, ch):
        if j == 2:
            return jnp.logical_and(z_lo == 1, y == 1)
        last = jnp.logical_or(y == 1, y == 2) if j == 1 else y == 0
        return jnp.where(z_lo == 0, relays(j, ch), last)

    def build(lag, carry):
        t0 = table[pl.ds(2 * lag, 1), :]
        t1 = table[pl.ds(2 * lag + 1, 1), :]
        rows = pl.ds(pl.multiple_of(lag * BS, BS), BS)
        for g in range(HALF // BS):
            re = turned[0, :, pl.ds(g * BS, BS)]
            im = turned[1, :, pl.ds(g * BS, BS)]
            left[rows, pl.ds(g * BS, BS)] = (t0 * re + t1 * im).astype(jnp.bfloat16)
            left[rows, pl.ds(HALF + g * BS, BS)] = (t0 * im - t1 * re).astype(jnp.bfloat16)
        return carry

    def turn(g, carry):
        rows = pl.ds(pl.multiple_of(g * BS, BS), BS)
        for r in range(2):
            turned[r, :, rows] = blocks[0, pl.ds(pl.multiple_of(r * HALF + g * BS, BS), BS), :].astype(jnp.float32).T
        return carry

    lax.fori_loop(0, HALF // BS, turn, 0)
    table_copy.wait()
    lax.fori_loop(0, LAGS // 2, build, 0)

    for s in range(CHUNKS):
        @pl.when(z_lo == 0)
        def _(s=s):
            take_far(s)
        take(1, s, early(1, s) if s < CHUNKS // 2 else jnp.logical_and(early(1, s), jnp.logical_not(jnp.logical_or(waits, y >= 3 - (z_lo == 0).astype(jnp.int32)))))
        take(3, own_turn[s], jnp.logical_and(z_lo == 1, early(3, own_turn[s])))
        if s > 0:
            take(3, s - 1, jnp.logical_and(z_lo == 0, jnp.logical_and(relays(3, s - 1), y != 1)))
        if s == CHUNKS // 2 - 1:
            @pl.when(held)
            def _():
                for ch in upper:
                    near(1, ch).start()
        lax.fori_loop(LAGS // 2 + s * LAGS // 8, LAGS // 2 + (s + 1) * LAGS // 8, build, 0)

    @pl.when(y == 3)
    def _():
        around().wait_recv()
        around_on().start()

    def sibling_done(j):
        for ch in range(CHUNKS):
            across(j, ch).wait_recv()

    @pl.when(z_lo == 1)
    def _():
        for ch in range(CHUNKS):
            take(2, ch, early(2, ch))
        for j in range(4):
            @pl.when(jnp.logical_and(core == 0, y == 3 - j))
            def _(j=j):
                sibling_done(j)

    def pass_on(ch, yy):
        take(3, ch, jnp.logical_and(z_lo == 0, y == yy))

    def take_late(j, ch):
        take(j, ch, jnp.logical_not(early(j, ch)))

    def gather_rest():
        @pl.when(jnp.logical_and(z_lo == 1, y == 3))
        def _():
            for ch in upper:
                aside(ch).wait_recv()
                aside_on(ch).start()

        for j in (1, 3, 2):
            for ch in range(CHUNKS):
                take_late(j, ch)
        for j in range(4):
            taken = jnp.logical_and(z_lo == 1, jnp.logical_and(core == 0, y == 3 - j))

            @pl.when(jnp.logical_and(chip + j + core <= 7, jnp.logical_not(taken)))
            def _(j=j):
                sibling_done(j)

    def pieces_of(k):
        return 2 if k == K - 1 else 1

    def hop(k, way, kind, piece=0):
        rows, rest = HX // pieces_of(k), TAIL if kind == 2 else 0
        used = pl.ds(0, HX) if kind == 0 else pl.ds(piece * (rows + rest), rows + rest)
        return remote(
            go.at[k, way, kind, used], come.at[k, way, kind, used],
            x_send.at[k, way, kind, piece], x_recv.at[k, way, kind, piece], x_down if way else x_up,
        )

    def hops_of(k):
        return [(0, 0)] + [(kind, piece) for kind in (1, 2) for piece in range(pieces_of(k))]

    def z_copy(k, ee):
        return remote(
            zsums.at[k, ee - 1], zgot.at[k, ee - 1], z_send.at[k, ee - 1], z_recv.at[k, ee - 1],
            at_band(x, (z_hi + ee) % 4),
        )

    square = (BS, BS)
    diagonal = lax.broadcasted_iota(jnp.int32, square, 0) == lax.broadcasted_iota(jnp.int32, square, 1)
    tail_row = lax.broadcasted_iota(jnp.int32, (TAIL, BS), 0)

    def pack(message, lags, value_of):
        tail = jnp.zeros((TAIL, BS), jnp.float32)
        for lag in range(lags):
            value = value_of(lag)
            rounded = value.astype(jnp.bfloat16)
            message[pl.ds(lag * BS, BS), :] = rounded
            rest = jnp.where(diagonal, value - rounded.astype(jnp.float32), 0.0)
            tail = jnp.where(tail_row == lag, jnp.sum(rest, axis=0, keepdims=True), tail)
        message[pl.ds(lags * BS, TAIL), :] = tail.astype(jnp.bfloat16)

    def plain(message, value_of):
        for lag in range(4):
            message[pl.ds(lag * BS, BS), :] = value_of(lag).astype(jnp.bfloat16)

    def unpack(message, lags, lag):
        tail = message[pl.ds(lags * BS, TAIL), :].astype(jnp.float32)[lag:lag + 1]
        return message[pl.ds(lag * BS, BS), :].astype(jnp.float32) + jnp.where(diagonal, tail, 0.0)

    def rows_at(place):
        return pl.ds(pl.multiple_of(place * BS, BS), BS)

    def send_middle(k, way):
        plain(go.at[k, way, 0], lambda lag: part[k, 0, rows_at(way * 4 + lag), :])
        hop(k, way, 0).start()

    def sent(k, kind):
        for way in (0, 1):
            hop(k, way, kind).wait_send()

    def send_straight(k, way, piece=0):
        if piece == 0:
            plain(go.at[k, way, 1], lambda lag: part[k, 1 + way, rows_at((1 - way) * 4 + lag), :])
        hop(k, way, 1, piece).start()

    def send_summed(k, piece=0):
        count = 4 // pieces_of(k)
        size = HX // pieces_of(k) + TAIL
        for way in (0, 1):
            def both(lag, way=way):
                at = piece * count + lag
                through = come[k, way, 0, rows_at(at), :].astype(jnp.float32)
                return part[k, 1 + way, rows_at(way * 4 + at), :] + through

            if piece == 0:
                hop(k, way, 0).wait_recv()
            pack(go.at[k, way, 2, pl.ds(piece * size, size)], count, both)
            hop(k, way, 2, piece).start()

    def reduce_x(k):
        count = 4 // pieces_of(k)
        size = HX // pieces_of(k) + TAIL
        for piece in range(pieces_of(k)):
            for way in (0, 1):
                hop(k, way, 1, piece).wait_recv()
                hop(k, way, 2, piece).wait_recv()
            for way in (0, 1):
                for lag in range(count):
                    at = piece * count + lag
                    rows = rows_at(way * 4 + at)
                    straight = come[k, 1 - way, 1, rows_at(at), :].astype(jnp.float32)
                    summed = unpack(come.at[k, way, 2, pl.ds(piece * size, size)], count, lag)
                    part[k, 3, rows, :] = part[k, 3, rows, :] + straight + summed
            if pieces_of(k) == 1:
                for ee in (2, 1, 3):
                    send_z(k, ee)
            else:
                for e in (piece, 2 + piece):
                    @pl.when(e != z_hi)
                    def _(e=e):
                        send_z(k, (e + 4 - z_hi) % 4)

    def send_z(k, ee):
        e = (z_hi + ee) % 4
        pack(zsums.at[k, ee - 1], 2, lambda lag: part[k, 3, rows_at(e * 2 + lag), :])
        z_copy(k, ee).start()

    def give(lag, k):
        return pltpu.make_async_copy(done.at[lag, k], out.at[lag, 0, k], done_sem.at[lag, k])

    def finish(k):
        for ee in (1, 3, 2):
            z_copy(k, ee).wait_recv()
        for lag in range(2):
            total = part[k, 3, rows_at(z_hi * 2 + lag), :]
            for s in range(3):
                total += unpack(zgot.at[k, s], 2, lag)
            done[lag, k] = (total * SCALE).astype(jnp.bfloat16)
            give(lag, k).start()

    def pick(t, values):
        chosen = jnp.int32(values[-1])
        for at in range(len(values) - 1):
            chosen = jnp.where(t == at, values[at], chosen)
        return chosen

    def multiply(slots, *after):
        width = len(slots) * BS

        def step(t, carry):
            q = pick(t, (0, 0, 1, 2, 1, 2, 3, 3))
            high = pick(t, (0, 1, 1, 0, 0, 1, 0, 1))
            ahead = pick(t, (2, 2, 1, 3, 1, 3, 0, 0))
            rows = pl.ds(pl.multiple_of(((x + ahead) % 4 * 2 + high) * HX, HX), HX)
            total = jnp.dot(left[rows, :], right[:, pl.ds(0, width)], preferred_element_type=jnp.float32)
            for n, k in enumerate(slots):
                part[k, q, pl.ds(pl.multiple_of(high * HX, HX), HX), :] = total[:, n * BS:(n + 1) * BS]
            for at, then in enumerate(after):
                pl.when(t == at)(then)
            return carry

        lax.fori_loop(0, 8, step, 0)

    def run(*steps):
        def then():
            for step in steps:
                step[0](*step[1:])

        return then

    right[:, pl.ds(0, BS)] = blocks[jnp.minimum(REACH, 15 - fibre)]
    multiply(
        (0,),
        run((send_middle, 0, 0), (pass_on, 3, 0), (take, 1, 2, jnp.logical_and(z_lo == 0, y >= 2))),
        run((send_middle, 0, 1), (pass_on, 3, 2), (take, 1, 2, waits)),
        run((send_straight, 0, 0)),
        run((send_straight, 0, 1), (pass_on, 3, 1), (take, 1, 3, waits)),
        run(),
        run(),
        run(),
        run((send_summed, 0)),
    )
    gather_rest()
    for n, slot in enumerate((1, 2)):
        right[:, pl.ds(n * BS, BS)] = blocks[offsets[0, slot]]
    multiply(
        (1, 2),
        run((send_middle, 1, 0)),
        run((send_middle, 1, 1)),
        run((send_straight, 1, 0)),
        run((send_straight, 1, 1)),
        run((send_middle, 2, 0), (send_middle, 2, 1)),
        run(),
        run((send_summed, 1)),
        run((send_straight, 2, 0), (send_straight, 2, 1), (reduce_x, 0)),
    )
    right[:, pl.ds(0, BS)] = blocks[offsets[0, 3]]
    multiply(
        (3,),
        run(),
        run((send_summed, 2), (reduce_x, 1), (sent, 2, 1), (send_middle, 3, 0), (send_middle, 3, 1)),
        run(),
        run((send_straight, 3, 0), (send_straight, 3, 1)),
        run((sent, 2, 2), (reduce_x, 2)),
        run(),
        run((finish, 0)),
        run((send_summed, 3, 0), (send_straight, 3, 0, 1), (send_straight, 3, 1, 1), (send_summed, 3, 1)),
    )
    finish(1)
    reduce_x(3)
    finish(2)
    finish(3)

    @pl.when(y >= 2)
    def _():
        around().wait_send()

    @pl.when(jnp.logical_and(z_lo == 1, y >= 2))
    def _():
        for ch in upper:
            aside(ch).wait_send()

    @pl.when(z_lo == 1)
    def _():
        for ch in range(CHUNKS):
            far(ch).wait_send()

    for j in (1, 3):
        for ch in range(CHUNKS):
            @pl.when(near_goes(j, ch))
            def _(j=j, ch=ch):
                near(j, ch).wait_send()

            @pl.when(relays(j, ch))
            def _(j=j, ch=ch):
                relay(j, ch).wait_send()

    for j in range(4):
        @pl.when(chip + j + (1 - core) <= 7)
        def _(j=j):
            for ch in range(CHUNKS):
                across(j, ch).wait_send()

    for k in range(K):
        for way in (0, 1):
            for kind, piece in hops_of(k):
                if k != 2 or kind == 0:
                    hop(k, way, kind, piece).wait_send()
        for ee in (1, 2, 3):
            z_copy(k, ee).wait_send()
        for lag in range(2):
            give(lag, k).wait()


def on_device(spectra, dead_mask, partner_offset):
    vmem = pl.BlockSpec(memory_space=pltpu.VMEM)
    bf16, f32 = jnp.bfloat16, jnp.float32
    return pl.pallas_call(
        kernel,
        out_shape=jax.ShapeDtypeStruct((LAGS // BANDS, 1, K, BS, BS), bf16),
        in_specs=[pl.BlockSpec(memory_space=pl.ANY), vmem, pl.BlockSpec(memory_space=pltpu.SMEM), pl.BlockSpec(memory_space=pl.ANY)],
        out_specs=pl.BlockSpec(memory_space=pl.ANY),
        scratch_shapes=[
            pltpu.VMEM((DEPTH, BS), bf16),
            pltpu.VMEM((LAGS // BANDS, K, BS, BS), bf16),
            pltpu.SemaphoreType.DMA,
            pltpu.SemaphoreType.DMA((LAGS // BANDS, K)),
            pltpu.VMEM((REACH + 1, DEPTH, BS), bf16),
            pltpu.VMEM((CROWS, BS), bf16),
            pltpu.VMEM((2, BS, HALF), f32),
            pltpu.VMEM((LAGS * BS, DEPTH), bf16),
            pltpu.VMEM((DEPTH, 2 * BS), bf16),
            pltpu.VMEM((2 * LAGS, BS), f32),
            pltpu.VMEM((K, 4, XROWS, BS), f32),
            pltpu.VMEM((K, 2, 3, HX + 2 * TAIL, BS), bf16),
            pltpu.VMEM((K, 2, 3, HX + 2 * TAIL, BS), bf16),
            pltpu.VMEM((K, 3, ZROWS + TAIL, BS), bf16),
            pltpu.VMEM((K, 3, ZROWS + TAIL, BS), bf16),
            pltpu.SemaphoreType.DMA,
            pltpu.SemaphoreType.DMA((4, CHUNKS)),
            pltpu.SemaphoreType.DMA((2, CHUNKS)),
            pltpu.SemaphoreType.DMA((CHUNKS,)),
            pltpu.SemaphoreType.DMA,
            pltpu.SemaphoreType.DMA,
            pltpu.SemaphoreType.DMA((REACH + 1, CHUNKS)),
            pltpu.SemaphoreType.DMA((4, CHUNKS)),
            pltpu.SemaphoreType.DMA((K, 2, 3, 2)),
            pltpu.SemaphoreType.DMA((K, 2, 3, 2)),
            pltpu.SemaphoreType.DMA((K, 3)),
            pltpu.SemaphoreType.DMA((K, 3)),
        ],
        compiler_params=pltpu.CompilerParams(
            collective_id=0, has_side_effects=True, vmem_limit_bytes=56 * 1024 * 1024
        ),
        cost_estimate=pl.CostEstimate(
            flops=2 * LAGS * BS * DEPTH * K * BS, bytes_accessed=1 << 20, transcendentals=0
        ),
    )(spectra.reshape(DEPTH, BS), dead_mask.reshape(1, BS), partner_offset, jnp.asarray(lag_table()))


def solution(mesh):
    in_specs = (P(None, None, "band", "fibre"), P("fibre"), P("fibre", None))
    out_specs = P("band", "fibre", None, None, None)
    return jax.shard_map(
        on_device, mesh=mesh, in_specs=in_specs, out_specs=out_specs, check_vma=False
    )
```

```python
import functools
import math

import jax
import jax.numpy as jnp
import ml_dtypes
import numpy as np
from jax import lax
from jax.experimental import pallas as pl
from jax.experimental.pallas import tpu as pltpu
from jax.sharding import PartitionSpec as P

BS = 128
NF = 512
REACH = 8
K = 4
W = 32
LAGS = 32
BANDS = 16
BINS = NF // BANDS
DEPTH = 2 * W * BINS
HALF = W * BINS
CHUNKS = 4
CROWS = DEPTH // CHUNKS
XROWS = LAGS // 4 * BS
HX = XROWS // 2
ZROWS = LAGS // 16 * BS
TAIL = 16
SCALE = 1.0 / math.sqrt(W) / math.sqrt(NF)


def lag_table():
    bins = np.arange(NF)[:, None]
    lags = np.arange(LAGS)[None, :] - LAGS // 2
    angles = (bins * lags % (2 * NF)) * (math.pi / NF)
    table = np.stack([np.cos(angles), -np.sin(angles)], axis=2)
    table = table.astype(np.float32).astype(ml_dtypes.bfloat16).astype(np.float32)
    table = table.reshape(BANDS, BINS, 2 * LAGS).transpose(0, 2, 1)
    return np.tile(table, (1, 1, BS // BINS))


def kernel(
    spectra, mask, offsets, tables, out,
    raw, done, raw_sem, done_sem, blocks, spare, turned, left, right, table, part, go, come, zsums, zgot,
    table_sem, gather_send, relay_send, aside_send, around_send, around_recv, gather_recv, sib_send, x_send, x_recv, z_send, z_recv,
):
    fibre, band = lax.axis_index("fibre"), lax.axis_index("band")
    z_lo, y, core = fibre // 8, fibre // 2 % 4, fibre % 2
    chip = fibre // 2
    x, z_hi = band // 4, band % 4

    def at_fibre(zz, yy, cc):
        return {"fibre": (zz * 4 + yy) * 2 + cc, "band": band}

    def at_band(xx, zz):
        return {"fibre": fibre, "band": xx * 4 + zz}

    sibling = at_fibre(z_lo, y, 1 - core)
    other_z = at_fibre(1 - z_lo, y, core)
    y_down, y_up = at_fibre(z_lo, (y + 3) % 4, core), at_fibre(z_lo, (y + 1) % 4, core)
    x_down, x_up = at_band((x + 3) % 4, z_hi), at_band((x + 1) % 4, z_hi)
    raw_copy = pltpu.make_async_copy(spectra, raw, raw_sem)
    raw_copy.start()
    barrier = pltpu.get_barrier_semaphore()
    peers = [sibling, other_z, y_down, y_up, x_down, x_up]
    peers += [at_band(x, (z_hi + j) % 4) for j in (1, 2, 3)]
    for peer in peers:
        pl.semaphore_signal(barrier, inc=1, device_id=peer, device_id_type=pl.DeviceIdType.MESH)

    table_copy = pltpu.make_async_copy(tables.at[band], table, table_sem)
    table_copy.start()
    alive = mask[...].astype(jnp.bfloat16)
    raw_copy.wait()
    blocks[0] = raw[...] * alive
    pl.semaphore_wait(barrier, len(peers))

    def remote(src, dst, send, recv, device):
        return pltpu.make_async_remote_copy(
            src_ref=src, dst_ref=dst, send_sem=send, recv_sem=recv,
            device_id=device, device_id_type=pl.DeviceIdType.MESH,
        )

    def rows_of(ch):
        return pl.ds(ch * CROWS, CROWS)

    def far(ch):
        return remote(
            blocks.at[0, rows_of(ch)], blocks.at[8, rows_of(ch)],
            gather_send.at[0, ch], gather_recv.at[8, ch], other_z,
        )

    def near(j, ch):
        src = jnp.where(y >= j, 0, 8)
        return remote(
            blocks.at[src, rows_of(ch)], blocks.at[2 * j, rows_of(ch)],
            gather_send.at[j, ch], gather_recv.at[2 * j, ch], y_down if j == 1 else y_up,
        )

    def relay(j, ch):
        return remote(
            blocks.at[2 * j, rows_of(ch)], blocks.at[4, rows_of(ch)],
            relay_send.at[j // 2, ch], gather_recv.at[4, ch], y_down if j == 1 else y_up,
        )

    def across(j, ch):
        return remote(
            blocks.at[2 * j + 2 * (1 - core), rows_of(ch)], blocks.at[2 * j + 1, rows_of(ch)],
            sib_send.at[j, ch], gather_recv.at[2 * j + 1, ch], sibling,
        )

    def aside(ch):
        return remote(
            blocks.at[0, rows_of(ch)], blocks.at[8, rows_of(ch)],
            aside_send.at[ch], gather_recv.at[8, ch], y_up,
        )

    def aside_on(ch):
        return remote(
            blocks.at[8, rows_of(ch)], blocks.at[6, rows_of(ch)],
            aside_send.at[ch], gather_recv.at[6, ch], other_z,
        )

    upper = range(CHUNKS // 2, CHUNKS)
    last_rows = rows_of(CHUNKS - 1)

    def around():
        return remote(blocks.at[0, last_rows], spare, around_send, around_recv, y_up)

    def around_on():
        return remote(spare, blocks.at[4, last_rows], around_send, gather_recv.at[4, CHUNKS - 1], y_up)

    def relays(j, ch):
        last = ch == CHUNKS - 1
        low = z_lo == 0
        if j == 1:
            goes = [jnp.logical_and(y >= 1, not last)]
            if ch == 2:
                goes = [jnp.logical_or(y == 1, jnp.logical_and(low, y >= 2))]
        else:
            goes = [y == 2, jnp.logical_and(y == 0, jnp.logical_or(last, jnp.logical_and(ch == 2, jnp.logical_not(low))))]
            goes.append(jnp.logical_and(y == 1, last))
        goes = functools.reduce(jnp.logical_or, goes)
        return jnp.logical_and(chip + j <= 7, goes)

    def near_goes(j, ch):
        limit = 1 if j == 1 else 2 if ch in upper else 3
        return jnp.logical_or(y >= j, jnp.logical_and(z_lo == 0, y < limit))

    @pl.when(z_lo == 1)
    def _():
        for ch in range(CHUNKS):
            far(ch).start()

    own_turn = [*upper, *range(CHUNKS // 2)]
    held = jnp.logical_and(z_lo == 1, y == 2)
    waits = jnp.logical_and(z_lo == 1, y == 1)

    @pl.when(y >= 1)
    def _():
        for ch in range(CHUNKS // 2):
            near(1, ch).start()

    @pl.when(jnp.logical_and(y >= 1, jnp.logical_not(held)))
    def _():
        for ch in upper:
            near(1, ch).start()

    @pl.when(y == 3)
    def _():
        for ch in own_turn:
            near(3, ch).start()

    @pl.when(y == 2)
    def _():
        around().start()

    @pl.when(core == 1)
    def _():
        for ch in range(CHUNKS):
            across(0, ch).start()

    @pl.when(jnp.logical_and(z_lo == 1, y == 2))
    def _():
        for ch in upper:
            aside(ch).start()

    def take_far(ch):
        far(ch).wait_recv()
        for j in (1, 3):
            @pl.when(jnp.logical_and(y < j, near_goes(j, ch)))
            def _(j=j):
                near(j, ch).start()

        @pl.when(core == 0)
        def _():
            across(3, ch).start()

    def take(j, ch, when):
        @pl.when(jnp.logical_and(chip + j <= 7, when))
        def _():
            remote(
                blocks.at[0, rows_of(ch)], blocks.at[2 * j, rows_of(ch)],
                gather_send.at[0, ch], gather_recv.at[2 * j, ch], y_up,
            ).wait_recv()
            if j != 2:
                @pl.when(relays(j, ch))
                def _():
                    relay(j, ch).start()
            across(j - 1 + core, ch).start()

    def early(j, ch):
        if j == 2:
            return jnp.logical_and(z_lo == 1, y == 1)
        last = jnp.logical_or(y == 1, y == 2) if j == 1 else y == 0
        return jnp.where(z_lo == 0, relays(j, ch), last)

    def build(lag, carry):
        t0 = table[pl.ds(2 * lag, 1), :]
        t1 = table[pl.ds(2 * lag + 1, 1), :]
        rows = pl.ds(pl.multiple_of(lag * BS, BS), BS)
        for g in range(HALF // BS):
            re = turned[0, :, pl.ds(g * BS, BS)]
            im = turned[1, :, pl.ds(g * BS, BS)]
            left[rows, pl.ds(g * BS, BS)] = (t0 * re + t1 * im).astype(jnp.bfloat16)
            left[rows, pl.ds(HALF + g * BS, BS)] = (t0 * im - t1 * re).astype(jnp.bfloat16)
        return carry

    def turn(g, carry):
        rows = pl.ds(pl.multiple_of(g * BS, BS), BS)
        for r in range(2):
            turned[r, :, rows] = blocks[0, pl.ds(pl.multiple_of(r * HALF + g * BS, BS), BS), :].astype(jnp.float32).T
        return carry

    lax.fori_loop(0, HALF // BS, turn, 0)
    table_copy.wait()
    lax.fori_loop(0, LAGS // 2, build, 0)

    for s in range(CHUNKS):
        @pl.when(z_lo == 0)
        def _(s=s):
            take_far(s)
        take(1, s, early(1, s) if s < CHUNKS // 2 else jnp.logical_and(early(1, s), jnp.logical_not(jnp.logical_or(waits, y >= 3 - (z_lo == 0).astype(jnp.int32)))))
        take(3, own_turn[s], jnp.logical_and(z_lo == 1, early(3, own_turn[s])))
        if s > 0:
            take(3, s - 1, jnp.logical_and(z_lo == 0, jnp.logical_and(relays(3, s - 1), y != 1)))
        if s == CHUNKS // 2 - 1:
            @pl.when(held)
            def _():
                for ch in upper:
                    near(1, ch).start()
        lax.fori_loop(LAGS // 2 + s * LAGS // 8, LAGS // 2 + (s + 1) * LAGS // 8, build, 0)

    @pl.when(y == 3)
    def _():
        around().wait_recv()
        around_on().start()

    def sibling_done(j):
        for ch in range(CHUNKS):
            across(j, ch).wait_recv()

    @pl.when(z_lo == 1)
    def _():
        for ch in range(CHUNKS):
            take(2, ch, early(2, ch))
        for j in range(4):
            @pl.when(jnp.logical_and(core == 0, y == 3 - j))
            def _(j=j):
                sibling_done(j)

    def pass_on(ch, yy):
        take(3, ch, jnp.logical_and(z_lo == 0, y == yy))

    def take_late(j, ch):
        take(j, ch, jnp.logical_not(early(j, ch)))

    def gather_rest():
        @pl.when(jnp.logical_and(z_lo == 1, y == 3))
        def _():
            for ch in upper:
                aside(ch).wait_recv()
                aside_on(ch).start()

        for j in (1, 3, 2):
            for ch in range(CHUNKS):
                take_late(j, ch)
        for j in range(4):
            taken = jnp.logical_and(z_lo == 1, jnp.logical_and(core == 0, y == 3 - j))

            @pl.when(jnp.logical_and(chip + j + core <= 7, jnp.logical_not(taken)))
            def _(j=j):
                sibling_done(j)

    def pieces_of(k):
        return 2 if k == K - 1 else 1

    def hop(k, way, kind, piece=0):
        rows, rest = HX // pieces_of(k), TAIL if kind == 2 else 0
        used = pl.ds(0, HX) if kind == 0 else pl.ds(piece * (rows + rest), rows + rest)
        return remote(
            go.at[k, way, kind, used], come.at[k, way, kind, used],
            x_send.at[k, way, kind, piece], x_recv.at[k, way, kind, piece], x_down if way else x_up,
        )

    def hops_of(k):
        return [(0, 0)] + [(kind, piece) for kind in (1, 2) for piece in range(pieces_of(k))]

    def z_copy(k, ee):
        return remote(
            zsums.at[k, ee - 1], zgot.at[k, ee - 1], z_send.at[k, ee - 1], z_recv.at[k, ee - 1],
            at_band(x, (z_hi + ee) % 4),
        )

    square = (BS, BS)
    diagonal = lax.broadcasted_iota(jnp.int32, square, 0) == lax.broadcasted_iota(jnp.int32, square, 1)
    tail_row = lax.broadcasted_iota(jnp.int32, (TAIL, BS), 0)

    def pack(message, lags, value_of):
        tail = jnp.zeros((TAIL, BS), jnp.float32)
        for lag in range(lags):
            value = value_of(lag)
            rounded = value.astype(jnp.bfloat16)
            message[pl.ds(lag * BS, BS), :] = rounded
            rest = jnp.where(diagonal, value - rounded.astype(jnp.float32), 0.0)
            tail = jnp.where(tail_row == lag, jnp.sum(rest, axis=0, keepdims=True), tail)
        message[pl.ds(lags * BS, TAIL), :] = tail.astype(jnp.bfloat16)

    def plain(message, value_of):
        for lag in range(4):
            message[pl.ds(lag * BS, BS), :] = value_of(lag).astype(jnp.bfloat16)

    def unpack(message, lags, lag):
        tail = message[pl.ds(lags * BS, TAIL), :].astype(jnp.float32)[lag:lag + 1]
        return message[pl.ds(lag * BS, BS), :].astype(jnp.float32) + jnp.where(diagonal, tail, 0.0)

    def rows_at(place):
        return pl.ds(pl.multiple_of(place * BS, BS), BS)

    def send_middle(k, way):
        plain(go.at[k, way, 0], lambda lag: part[k, 0, rows_at(way * 4 + lag), :])
        hop(k, way, 0).start()

    def sent(k, kind):
        for way in (0, 1):
            hop(k, way, kind).wait_send()

    def send_straight(k, way, piece=0):
        if piece == 0:
            plain(go.at[k, way, 1], lambda lag: part[k, 1 + way, rows_at((1 - way) * 4 + lag), :])
        hop(k, way, 1, piece).start()

    def send_summed(k, piece=0):
        count = 4 // pieces_of(k)
        size = HX // pieces_of(k) + TAIL
        for way in (0, 1):
            def both(lag, way=way):
                at = piece * count + lag
                through = come[k, way, 0, rows_at(at), :].astype(jnp.float32)
                return part[k, 1 + way, rows_at(way * 4 + at), :] + through

            if piece == 0:
                hop(k, way, 0).wait_recv()
            pack(go.at[k, way, 2, pl.ds(piece * size, size)], count, both)
            hop(k, way, 2, piece).start()

    def reduce_x(k):
        count = 4 // pieces_of(k)
        size = HX // pieces_of(k) + TAIL
        for piece in range(pieces_of(k)):
            for way in (0, 1):
                hop(k, way, 1, piece).wait_recv()
                hop(k, way, 2, piece).wait_recv()
            for way in (0, 1):
                for lag in range(count):
                    at = piece * count + lag
                    rows = rows_at(way * 4 + at)
                    straight = come[k, 1 - way, 1, rows_at(at), :].astype(jnp.float32)
                    summed = unpack(come.at[k, way, 2, pl.ds(piece * size, size)], count, lag)
                    part[k, 3, rows, :] = part[k, 3, rows, :] + straight + summed
            if pieces_of(k) == 1:
                for ee in (2, 1, 3):
                    send_z(k, ee)
            else:
                for e in (piece, 2 + piece):
                    @pl.when(e != z_hi)
                    def _(e=e):
                        send_z(k, (e + 4 - z_hi) % 4)

    def send_z(k, ee):
        e = (z_hi + ee) % 4
        pack(zsums.at[k, ee - 1], 2, lambda lag: part[k, 3, rows_at(e * 2 + lag), :])
        z_copy(k, ee).start()

    def give(lag, k):
        return pltpu.make_async_copy(done.at[lag, k], out.at[lag, 0, k], done_sem.at[lag, k])

    def finish(k):
        for ee in (1, 3, 2):
            z_copy(k, ee).wait_recv()
        for lag in range(2):
            total = part[k, 3, rows_at(z_hi * 2 + lag), :]
            for s in range(3):
                total += unpack(zgot.at[k, s], 2, lag)
            done[lag, k] = (total * SCALE).astype(jnp.bfloat16)
            give(lag, k).start()

    def pick(t, values):
        chosen = jnp.int32(values[-1])
        for at in range(len(values) - 1):
            chosen = jnp.where(t == at, values[at], chosen)
        return chosen

    def multiply(slots, *after):
        width = len(slots) * BS

        def step(t, carry):
            q = pick(t, (0, 0, 1, 2, 1, 2, 3, 3))
            high = pick(t, (0, 1, 1, 0, 0, 1, 0, 1))
            ahead = pick(t, (2, 2, 1, 3, 1, 3, 0, 0))
            rows = pl.ds(pl.multiple_of(((x + ahead) % 4 * 2 + high) * HX, HX), HX)
            total = jnp.dot(left[rows, :], right[:, pl.ds(0, width)], preferred_element_type=jnp.float32)
            for n, k in enumerate(slots):
                part[k, q, pl.ds(pl.multiple_of(high * HX, HX), HX), :] = total[:, n * BS:(n + 1) * BS]
            for at, then in enumerate(after):
                pl.when(t == at)(then)
            return carry

        lax.fori_loop(0, 8, step, 0)

    def run(*steps):
        def then():
            for step in steps:
                step[0](*step[1:])

        return then

    right[:, pl.ds(0, BS)] = blocks[jnp.minimum(REACH, 15 - fibre)]
    multiply(
        (0,),
        run((send_middle, 0, 0), (pass_on, 3, 0), (take, 1, 2, jnp.logical_and(z_lo == 0, y >= 2))),
        run((send_middle, 0, 1), (pass_on, 3, 2), (take, 1, 2, waits)),
        run((send_straight, 0, 0)),
        run((send_straight, 0, 1), (pass_on, 3, 1), (take, 1, 3, waits)),
        run(),
        run(),
        run(),
        run((send_summed, 0)),
    )
    gather_rest()
    for n, slot in enumerate((1, 2)):
        right[:, pl.ds(n * BS, BS)] = blocks[offsets[0, slot]]
    multiply(
        (1, 2),
        run((send_middle, 1, 0)),
        run((send_middle, 1, 1)),
        run((send_straight, 1, 0)),
        run((send_straight, 1, 1)),
        run((send_middle, 2, 0), (send_middle, 2, 1)),
        run((reduce_x, 0)),
        run((send_summed, 1)),
        run((send_straight, 2, 0), (send_straight, 2, 1)),
    )
    right[:, pl.ds(0, BS)] = blocks[offsets[0, 3]]
    multiply(
        (3,),
        run(),
        run((send_summed, 2), (reduce_x, 1), (sent, 2, 1), (send_middle, 3, 0), (send_middle, 3, 1)),
        run(),
        run((send_straight, 3, 0), (send_straight, 3, 1)),
        run((sent, 2, 2), (reduce_x, 2)),
        run(),
        run((finish, 0)),
        run((send_summed, 3, 0), (send_straight, 3, 0, 1), (send_straight, 3, 1, 1), (send_summed, 3, 1)),
    )
    finish(1)
    reduce_x(3)
    finish(2)
    finish(3)

    @pl.when(y >= 2)
    def _():
        around().wait_send()

    @pl.when(jnp.logical_and(z_lo == 1, y >= 2))
    def _():
        for ch in upper:
            aside(ch).wait_send()

    @pl.when(z_lo == 1)
    def _():
        for ch in range(CHUNKS):
            far(ch).wait_send()

    for j in (1, 3):
        for ch in range(CHUNKS):
            @pl.when(near_goes(j, ch))
            def _(j=j, ch=ch):
                near(j, ch).wait_send()

            @pl.when(relays(j, ch))
            def _(j=j, ch=ch):
                relay(j, ch).wait_send()

    for j in range(4):
        @pl.when(chip + j + (1 - core) <= 7)
        def _(j=j):
            for ch in range(CHUNKS):
                across(j, ch).wait_send()

    for k in range(K):
        for way in (0, 1):
            for kind, piece in hops_of(k):
                if k != 2 or kind == 0:
                    hop(k, way, kind, piece).wait_send()
        for ee in (1, 2, 3):
            z_copy(k, ee).wait_send()
        for lag in range(2):
            give(lag, k).wait()


def on_device(spectra, dead_mask, partner_offset):
    vmem = pl.BlockSpec(memory_space=pltpu.VMEM)
    bf16, f32 = jnp.bfloat16, jnp.float32
    return pl.pallas_call(
        kernel,
        out_shape=jax.ShapeDtypeStruct((LAGS // BANDS, 1, K, BS, BS), bf16),
        in_specs=[pl.BlockSpec(memory_space=pl.ANY), vmem, pl.BlockSpec(memory_space=pltpu.SMEM), pl.BlockSpec(memory_space=pl.ANY)],
        out_specs=pl.BlockSpec(memory_space=pl.ANY),
        scratch_shapes=[
            pltpu.VMEM((DEPTH, BS), bf16),
            pltpu.VMEM((LAGS // BANDS, K, BS, BS), bf16),
            pltpu.SemaphoreType.DMA,
            pltpu.SemaphoreType.DMA((LAGS // BANDS, K)),
            pltpu.VMEM((REACH + 1, DEPTH, BS), bf16),
            pltpu.VMEM((CROWS, BS), bf16),
            pltpu.VMEM((2, BS, HALF), f32),
            pltpu.VMEM((LAGS * BS, DEPTH), bf16),
            pltpu.VMEM((DEPTH, 2 * BS), bf16),
            pltpu.VMEM((2 * LAGS, BS), f32),
            pltpu.VMEM((K, 4, XROWS, BS), f32),
            pltpu.VMEM((K, 2, 3, HX + 2 * TAIL, BS), bf16),
            pltpu.VMEM((K, 2, 3, HX + 2 * TAIL, BS), bf16),
            pltpu.VMEM((K, 3, ZROWS + TAIL, BS), bf16),
            pltpu.VMEM((K, 3, ZROWS + TAIL, BS), bf16),
            pltpu.SemaphoreType.DMA,
            pltpu.SemaphoreType.DMA((4, CHUNKS)),
            pltpu.SemaphoreType.DMA((2, CHUNKS)),
            pltpu.SemaphoreType.DMA((CHUNKS,)),
            pltpu.SemaphoreType.DMA,
            pltpu.SemaphoreType.DMA,
            pltpu.SemaphoreType.DMA((REACH + 1, CHUNKS)),
            pltpu.SemaphoreType.DMA((4, CHUNKS)),
            pltpu.SemaphoreType.DMA((K, 2, 3, 2)),
            pltpu.SemaphoreType.DMA((K, 2, 3, 2)),
            pltpu.SemaphoreType.DMA((K, 3)),
            pltpu.SemaphoreType.DMA((K, 3)),
        ],
        compiler_params=pltpu.CompilerParams(
            collective_id=0, has_side_effects=True, vmem_limit_bytes=56 * 1024 * 1024
        ),
        cost_estimate=pl.CostEstimate(
            flops=2 * LAGS * BS * DEPTH * K * BS, bytes_accessed=1 << 20, transcendentals=0
        ),
    )(spectra.reshape(DEPTH, BS), dead_mask.reshape(1, BS), partner_offset, jnp.asarray(lag_table()))


def solution(mesh):
    in_specs = (P(None, None, "band", "fibre"), P("fibre"), P("fibre", None))
    out_specs = P("band", "fibre", None, None, None)
    return jax.shard_map(
        on_device, mesh=mesh, in_specs=in_specs, out_specs=out_specs, check_vma=False
    )
```
